256 devices in a mesh: seq: 32 (over z_lo, y, x), head: 8 (over z_hi, core).
Axes of the slice: x: 4, y: 4, z: 8 (z_hi: 4, z_lo: 2; z = z_hi * 2 + z_lo), core: 2. Of those that a mesh axis runs over, the one named last changes fastest.
Arguments:
- queries: bfloat16 [32768, 1024], P(('seq', 'head')), may hold values from -10 to 10, as said below
- keys: bfloat16 [32768, 1024], P(('seq', 'head')), may hold values from -8 to 8, as said below
- values: bfloat16 [32768, 1024], P(('seq', 'head')), may hold values from -6 to 6
- grad_out: bfloat16 [32768, 1024], P(('seq', 'head')), may hold values from -6 to 6
- doc_ids: int32 [32768], replicated, may hold values from 0 to 2, never falling along the last dimension, each value on 1 to 16384 neighbouring positions
Outputs:
- attended: bfloat16 [32768, 1024], P(('seq', 'head'))
- grad_queries: bfloat16 [32768, 1024], P(('seq', 'head'))
- grad_keys: bfloat16 [32768, 1024], P(('seq', 'head'))
- grad_values: bfloat16 [32768, 1024], P(('seq', 'head'))
The draws below stay inside these ranges and needn't reach their ends.
Inputs may be any that keep to these rules, and one draw needn't show every extreme that they name: `queries`: Real-valued entries. `keys`: Real-valued entries. `doc_ids`: document ids never fall along the sequence; the longest document holds exactly half of the 32768 tokens.
All inputs are finite; a program needn't handle non-finite values.
Results may differ from the reference program's by a relative error of at most 0.011.
Values may be sent and summed in bfloat16 or wider, within the bound.
A program may use at most 128 MiB of HBM per device.

```python
import math
import jax
import jax.numpy as jnp
import numpy as np
from jax import lax

HEADS = 16
HEAD_DIM = 64
D = 1024
DOCS = 3
SPARSE = 1024
TOKENS = 32768
N_SEQ = 32


def draw_queries(key, part):
    key = jax.random.fold_in(key, 7)
    return jnp.clip(2.5 * jax.random.normal(key, (TOKENS, D), jnp.float32), -10.0, 10.0).astype(jnp.bfloat16)


def draw_keys(key, part):
    key = jax.random.fold_in(key, 13)
    return jnp.clip(jax.random.normal(key, (TOKENS, D), jnp.float32), -6.0, 6.0).astype(jnp.bfloat16)


def level_of(key, dims, cuts, least, high):
    factor_of = 1.0
    for dim, parts in cuts:
        heights = jax.random.uniform(jax.random.fold_in(jax.random.fold_in(key, 6), dim), (parts,), jnp.float32, least / len(cuts), high / len(cuts))
        factor_of = factor_of * jnp.repeat(jnp.exp(heights), dims[dim] // parts).reshape((-1,) + (1,) * (len(dims) - 1 - dim))
    return factor_of


def length_profile(amount, total, reach, slope):
    weights = [(1 << 20) // math.isqrt(rank ** slope) + 1 for rank in range(2, amount + 1)]
    spare, holding = total - reach - (amount - 1), [1] * (amount - 1)
    while spare > 0:
        candidates = [i for i in range(amount - 1) if holding[i] < reach]
        whole, remaining = sum([weights[i] for i in candidates]), spare
        for i in candidates:
            more = min(reach - holding[i], max(1, remaining * weights[i] // whole), spare)
            holding[i] = holding[i] + more
            spare = spare - more
    return np.array([reach] + holding)


def uneven(rng, count, total, bound, skew):
    if count == 2:
        one = jax.random.randint(rng, (), max(1, total - bound), min(bound, total - 1) + 1)
        return jnp.stack([one, total - one])
    lengths = jnp.asarray(length_profile(count, total, bound, skew), jnp.int32)
    pairs = (count - 1) // 2
    source_of, sink = lengths[1:1 + 2 * pairs:2], lengths[2:2 + 2 * pairs:2]
    room = jnp.minimum(source_of - 1, bound - sink)
    moved = jax.random.randint(jax.random.fold_in(rng, 1), (pairs,), 0, 1 << 20) % (room + 1)
    lengths = lengths.at[1:1 + 2 * pairs:2].set(source_of - moved).at[2:2 + 2 * pairs:2].set(sink + moved)
    return lengths[jax.random.permutation(jax.random.fold_in(rng, 2), count)]


def gaussian(key, shape, deviation, reach, pieces=(), held_as=jnp.bfloat16):
    result = deviation * jax.random.normal(key, shape, jnp.float32)
    if pieces:
        result = result * level_of(key, shape, pieces, -0.22, 0.18)
    return jnp.clip(result, -reach, reach).astype(held_as)


def setup_inputs(seed: int = 0) -> dict:
    seeds = jax.random.split(jax.random.key(seed), 6)
    queries = draw_queries(jax.random.fold_in(seeds[5], 71), 0)
    keys = draw_keys(jax.random.fold_in(seeds[5], 71), 0)
    values = gaussian(seeds[2], (TOKENS, D), 1.0, 6.0, ((0, 256),))
    grad_out = gaussian(seeds[3], (TOKENS, D), 1.0, 6.0, ((0, 256),))
    doc_ids = jnp.searchsorted(jnp.cumsum(uneven(seeds[4], DOCS, TOKENS, TOKENS // 2, 0)), jnp.arange(TOKENS), side="right").astype(jnp.int32)
    return dict(queries=queries, keys=keys, values=values, grad_out=grad_out, doc_ids=doc_ids)


def level_rates():
    return [1, 2, 8, N_SEQ]


def visible_mask(segment_docs):
    return segment_docs[:, None] == segment_docs[None, :]


def segment_scores(query_rows, key_rows, segment_docs):
    scores = jnp.dot(query_rows, key_rows.T, preferred_element_type=jnp.float32) * HEAD_DIM ** -0.5
    return jnp.where(visible_mask(segment_docs), scores, -jnp.inf)


def segment_forward(segment_args):
    query_rows, key_rows, value_rows, segment_docs = segment_args
    scores = segment_scores(query_rows, key_rows, segment_docs)
    row_max = jnp.max(scores, axis=1)
    weights = jnp.exp(scores - row_max[:, None])
    row_total = jnp.sum(weights, axis=1)
    summed = jnp.dot(weights.astype(jnp.bfloat16), value_rows, preferred_element_type=jnp.float32)
    return row_max, row_total, summed


def segment_backward(segment_args):
    query_rows, key_rows, value_rows, upstream_rows, segment_docs, log_total, row_delta = segment_args
    scale = HEAD_DIM ** -0.5
    scores = segment_scores(query_rows, key_rows, segment_docs)
    probability = jnp.exp(scores - log_total[:, None])
    grad_values = jnp.dot(probability.astype(jnp.bfloat16).T, upstream_rows, preferred_element_type=jnp.float32)
    grad_scores = jnp.dot(upstream_rows, value_rows.T, preferred_element_type=jnp.float32)
    shifted = (probability * (grad_scores - row_delta[:, None])).astype(jnp.bfloat16)
    grad_queries = jnp.dot(shifted, key_rows, preferred_element_type=jnp.float32) * scale
    grad_keys = jnp.dot(shifted.T, query_rows, preferred_element_type=jnp.float32) * scale
    return grad_queries, grad_keys, grad_values


def reference(queries, keys, values, grad_out, doc_ids):
    attended_cols, query_cols, key_cols, value_cols = [], [], [], []
    for head_id in range(HEADS):
        columns = slice(head_id * HEAD_DIM, (head_id + 1) * HEAD_DIM)
        head_query = queries[:, columns]
        head_key = keys[:, columns]
        head_value = values[:, columns]
        head_upstream = grad_out[:, columns]
        row_max = jnp.full((TOKENS,), -jnp.inf, jnp.float32)
        row_total = jnp.zeros((TOKENS,), jnp.float32)
        summed = jnp.zeros((TOKENS, HEAD_DIM), jnp.float32)
        for dilation in level_rates():
            picked = slice(head_id % dilation, None, dilation)
            stats = lax.map(segment_forward, (
                head_query[picked].reshape(-1, SPARSE, HEAD_DIM),
                head_key[picked].reshape(-1, SPARSE, HEAD_DIM),
                head_value[picked].reshape(-1, SPARSE, HEAD_DIM),
                doc_ids[picked].reshape(-1, SPARSE)))
            level_max = stats[0].reshape(-1)
            level_total = stats[1].reshape(-1)
            level_sum = stats[2].reshape(-1, HEAD_DIM)
            old_max = row_max[picked]
            new_max = jnp.maximum(old_max, level_max)
            old_scale = jnp.exp(old_max - new_max)
            new_scale = jnp.exp(level_max - new_max)
            row_total = row_total.at[picked].set(row_total[picked] * old_scale + level_total * new_scale)
            summed = summed.at[picked].set(summed[picked] * old_scale[:, None] + level_sum * new_scale[:, None])
            row_max = row_max.at[picked].set(new_max)
        output = summed / row_total[:, None]
        log_total = row_max + jnp.log(row_total)
        row_delta = jnp.sum(head_upstream.astype(jnp.float32) * output, axis=1)
        grad_query = jnp.zeros((TOKENS, HEAD_DIM), jnp.float32)
        grad_key = jnp.zeros((TOKENS, HEAD_DIM), jnp.float32)
        grad_value = jnp.zeros((TOKENS, HEAD_DIM), jnp.float32)
        for dilation in level_rates():
            picked = slice(head_id % dilation, None, dilation)
            grads = lax.map(segment_backward, (
                head_query[picked].reshape(-1, SPARSE, HEAD_DIM),
                head_key[picked].reshape(-1, SPARSE, HEAD_DIM),
                head_value[picked].reshape(-1, SPARSE, HEAD_DIM),
                head_upstream[picked].reshape(-1, SPARSE, HEAD_DIM),
                doc_ids[picked].reshape(-1, SPARSE),
                log_total[picked].reshape(-1, SPARSE),
                row_delta[picked].reshape(-1, SPARSE)))
            grad_query = grad_query.at[picked].add(grads[0].reshape(-1, HEAD_DIM))
            grad_key = grad_key.at[picked].add(grads[1].reshape(-1, HEAD_DIM))
            grad_value = grad_value.at[picked].add(grads[2].reshape(-1, HEAD_DIM))
        attended_cols.append(output.astype(jnp.bfloat16))
        query_cols.append(grad_query.astype(jnp.bfloat16))
        key_cols.append(grad_key.astype(jnp.bfloat16))
        value_cols.append(grad_value.astype(jnp.bfloat16))
    return (jnp.concatenate(attended_cols, axis=1), jnp.concatenate(query_cols, axis=1),
            jnp.concatenate(key_cols, axis=1), jnp.concatenate(value_cols, axis=1))
```

```python
import jax
import jax.numpy as jnp
from jax import lax
from jax.experimental import pallas as pl
from jax.experimental.pallas import tpu as pltpu
from jax.sharding import PartitionSpec as P

F32 = jnp.float32
BF16 = jnp.bfloat16
I32 = jnp.int32
BIG = 1e30
NH = 8
NB = 128
MESH = pl.DeviceIdType.MESH


def iota(shape, dim):
    return lax.broadcasted_iota(I32, shape, dim)


def token_of(parity, w, h):
    t, u, a = (w >> 4) & 3, (w >> 2) & 3, w & 3
    return a * 32 + parity + 2 * ((h + t) & 3) + 8 * ((h // 4 + u) & 3)


def nn(a, b):
    return lax.dot_general(a, b, (((1,), (0,)), ((), ())), preferred_element_type=F32)


def attend_kernel(
    q_ref, k_ref, v_ref, do_ref, docs_ref, out_ref,
    send, inbuf, kv2, kv8, kv32, KX, KT, VT, VN, QG, QXT, QXT32, QM, DOM, DOT,
    ST, OT, DQT, ACC, g2, r2, g8, r8, g32, r32, g32z, r32z, og,
    in_ss, in_rs, loc_s, l2_ss, l2_rs, l8_ss, l8_rs, l32_ss, l32_rs, z_ss, z_rs, out_ss, out_rs,
):
    h = lax.axis_index("head")
    s = lax.axis_index("seq")
    pair = s + 1 - 2 * (s % 2)
    base8 = (s // 8) * 8
    base16 = (s // 16) * 16
    zpeer = (s + 16) % 32

    def plane_peer(k):
        return base16 + (s - base16 + k) % 16

    def oct_peer(k):
        return base8 + (s - base8 + k) % 8

    def head_peer(k):
        return (h + k) % NH

    barrier = pltpu.get_barrier_semaphore()
    for k in range(1, NH):
        pl.semaphore_signal(barrier, inc=1, device_id={"head": head_peer(k)}, device_id_type=MESH)
    for k in range(1, 16):
        pl.semaphore_signal(barrier, inc=1, device_id={"seq": plane_peer(k)}, device_id_type=MESH)
    pl.semaphore_signal(barrier, inc=1, device_id={"seq": zpeer}, device_id_type=MESH)

    lane = iota((64, 128), 1)
    low64 = lane < 64

    def permute_two(first, a_ref, b_ref):
        for g in range(NH):
            rho = iota((NB, NB), 0)
            mat = (iota((NB, NB), 1) == token_of(rho >> 6, rho & 63, g)).astype(F32).astype(BF16)
            cols = slice(g * 128, g * 128 + 128)
            both = jnp.concatenate([a_ref[:, cols], b_ref[:, cols]], axis=1)
            res = nn(mat, both)
            for i in range(2):
                even, odd = res[0:64, i * 128:i * 128 + 128], res[64:128, i * 128:i * 128 + 128]
                send[first + i, g, 0:64] = jnp.where(low64, even, odd).astype(BF16)
                send[first + i, g, 64:128] = jnp.where(low64, odd, even).astype(BF16)

    def in_copy(t, k):
        return pltpu.make_async_remote_copy(
            src_ref=send.at[t, head_peer(k)], dst_ref=inbuf.at[t, h],
            send_sem=in_ss.at[t * 7 + k - 1], recv_sem=in_rs.at[t * 7 + k - 1],
            device_id={"head": head_peer(k)}, device_id_type=MESH)

    def in_local(t):
        return pltpu.make_async_copy(send.at[t, h], inbuf.at[t, h], loc_s.at[t])

    def start_in(t):
        for k in range(1, NH):
            in_copy(t, k).start()
        in_local(t).start()

    def wait_in(t):
        for k in range(1, NH):
            in_copy(t, k).wait_recv()
        in_local(t).wait()

    permute_two(0, k_ref, v_ref)
    pl.semaphore_wait(barrier, 23)
    start_in(0)
    start_in(1)
    permute_two(2, q_ref, do_ref)
    start_in(2)
    start_in(3)

    docs = docs_ref[...]

    def count(limit):
        c = jnp.sum((docs < limit).astype(F32), axis=0, keepdims=True)
        return jnp.sum(c, axis=1, keepdims=True).astype(I32)

    bound1, bound2 = count(1), count(2)

    def doc_of(pos):
        return (pos >= bound1).astype(I32) + (pos >= bound2).astype(I32)

    lane128 = iota((128, 128), 1)
    row128 = iota((128, 128), 0)
    half = [lane128 < 64, lane128 >= 64]
    feat_lane = [lane128 - 64, lane128]
    half_row = [row128 < 64, row128 >= 64]
    feat_row = [row128 - 64, row128]

    def key_place(level, c):
        r = row128 + c * 128
        if level == 0:
            return s, r >> 7, r & 127
        if level == 1:
            return jnp.where((r >> 9) == 0, s, pair), (r >> 6) & 7, r & 63
        if level == 2:
            return base8 + ((s + (r >> 7)) & 7), (r >> 4) & 7, r & 15
        plane = jnp.where(((r >> 5) & 1) == 0, base16, 16 - base16)
        return plane + ((s + (r >> 6)) & 15), (r >> 2) & 7, r & 3

    def fill_features(c, carry):
        for level in range(4):
            seqs, src, w = key_place(level, c)
            start = seqs * 1024 + src * 128
            for j in range(2):
                parity = j ^ (w >> 6)
                doc = doc_of(start + token_of(parity, w & 63, h))
                hot = (feat_lane[j] == doc) | (feat_lane[j] == 3)
                KX[level, j, pl.ds(c * 128, 128)] = jnp.where(hot, 1.0, 0.0).astype(BF16)
        return carry

    lax.fori_loop(0, 8, fill_features, 0)

    for c in range(8):
        if c == 0:
            src, w = lane128 >> 4, lane128 & 15
        elif c < 4:
            i = lane128 + (c - 1) * 128
            src = (i * 1366) >> 16
            w = 16 + i - src * 48
        else:
            i = lane128 + (c - 4) * 128
            src, w = i >> 6, 64 + (i & 63)
        for j in range(2):
            parity = j ^ (w >> 6)
            doc = doc_of(s * 1024 + src * 128 + token_of(parity, w & 63, h))
            hide = (feat_row[j] >= 0) & (feat_row[j] < 3) & (feat_row[j] != doc)
            QXT[j, c] = jnp.where(hide, -BIG, 0.0).astype(BF16)
            if c == 0:
                hide = hide | ((feat_row[j] == 3) & (w >= 4))
                QXT32[j] = jnp.where(hide, -BIG, 0.0).astype(BF16)

    ACC[...] = jnp.zeros(ACC.shape, F32)

    wait_in(0)
    wait_in(1)
    l2_copy = pltpu.make_async_remote_copy(
        src_ref=inbuf.at[pl.ds(0, 2), :, pl.ds(0, 64), :], dst_ref=kv2.at[1],
        send_sem=l2_ss.at[0], recv_sem=l2_rs.at[0], device_id={"seq": pair}, device_id_type=MESH)
    l2_copy.start()

    pick_row, pick_col = iota((32, 128), 0), iota((32, 128), 1)
    pick = (pick_col == (pick_row >> 2) * 16 + (pick_row & 3)).astype(F32).astype(BF16)
    for t in range(2):
        kv32[0, 0, t] = nn(pick, inbuf[t, :, 0:16].reshape(128, 128)).astype(BF16)
    z_copy = pltpu.make_async_remote_copy(
        src_ref=kv32.at[0, 0], dst_ref=kv32.at[0, 1],
        send_sem=z_ss.at[0], recv_sem=z_rs.at[0], device_id={"seq": zpeer}, device_id_type=MESH)
    z_copy.start()

    def l8_copy(k):
        return pltpu.make_async_remote_copy(
            src_ref=inbuf.at[pl.ds(0, 2), :, pl.ds(0, 16), :], dst_ref=kv8.at[8 - k],
            send_sem=l8_ss.at[k - 1], recv_sem=l8_rs.at[k - 1], device_id={"seq": oct_peer(k)}, device_id_type=MESH)

    for k in range(1, 8):
        l8_copy(k).start()
    for t in range(2):
        kv2[0, t] = inbuf[t, :, 0:64]
        kv8[0, t] = inbuf[t, :, 0:16]

    def l32_copy(k):
        return pltpu.make_async_remote_copy(
            src_ref=kv32.at[0], dst_ref=kv32.at[16 - k],
            send_sem=l32_ss.at[k - 1], recv_sem=l32_rs.at[k - 1], device_id={"seq": plane_peer(k)}, device_id_type=MESH)

    def prepare(level, load):
        def chunk(c, carry):
            rows = pl.ds(pl.multiple_of(c * 128, 128), 128)
            key = load(0, c).astype(F32)
            val = load(1, c)
            for j in range(2):
                KX[level, j, rows] = jnp.where(half[j], key, KX[level, j, rows].astype(F32)).astype(BF16)
            KT[level, :, rows] = key.T.astype(BF16)
            VT[level, :, rows] = val.astype(F32).T.astype(BF16)
            VN[level, rows] = val
            return carry

        lax.fori_loop(0, 8, chunk, 0)

    prepare(0, lambda t, c: inbuf[t, c])

    z_copy.wait()
    for k in range(1, 16):
        l32_copy(k).start()

    def gather_order(t):
        x = inbuf.at[t]
        QG[0:128] = x[:, 0:16].reshape(128, 128)
        QG[128:512] = x[:, 16:64].reshape(384, 128)
        QG[512:1024] = x[:, 64:128].reshape(512, 128)

    wait_in(2)
    gather_order(2)
    for c in range(8):
        x = QG[c * 128:c * 128 + 128].astype(F32) * 0.125
        xt = x.T
        for j in range(2):
            QM[j, c * 128:c * 128 + 128] = jnp.where(half[j], x, 0.0).astype(BF16)
            QXT[j, c] = jnp.where(half_row[j], xt, QXT[j, c].astype(F32)).astype(BF16)
            if c == 0:
                QXT32[j] = jnp.where(half_row[j], xt, QXT32[j].astype(F32)).astype(BF16)

    def wide(ref, j, b):
        return jnp.concatenate([ref[j, 2 * b], ref[j, 2 * b + 1]], axis=1)

    def forward(level, j, qxt):
        sc = nn(KX[level, j], qxt)
        m = jnp.max(sc, axis=0, keepdims=True)
        w = jnp.exp(sc - m)
        total = jnp.sum(w, axis=0, keepdims=True)
        o = nn(VT[level, 64 * j:64 * j + 64], w.astype(BF16))
        return m, total, o

    def merge(j, b, width, m, total, o):
        m0, l0, o0 = ST[0, j, b, :, :width], ST[1, j, b, :, :width], OT[j, b, :, :width]
        mm = jnp.maximum(m0, m)
        e0, e1 = jnp.exp(m0 - mm), jnp.exp(m - mm)
        ST[0, j, b, :, :width] = mm
        ST[1, j, b, :, :width] = l0 * e0 + total * e1
        OT[j, b, :, :width] = o0 * e0 + o * e1

    def forward_first(b, carry):
        for j in range(2):
            m, total, o = forward(0, j, wide(QXT, j, b))
            ST[0, j, b] = m
            ST[1, j, b] = total
            OT[j, b] = o
        return carry

    lax.fori_loop(0, 4, forward_first, 0)

    l2_copy.wait()
    prepare(1, lambda t, c: kv2[c // 4, t, pl.ds((c % 4) * 2, 2)].reshape(128, 128))

    def forward_second(b, carry):
        for j in range(2):
            merge(j, b, 256, *forward(1, j, wide(QXT, j, b)))
        return carry

    lax.fori_loop(0, 2, forward_second, 0)

    for k in range(1, 8):
        l8_copy(k).wait()
    prepare(2, lambda t, c: kv8[c, t].reshape(128, 128))
    for j in range(2):
        merge(j, 0, 128, *forward(2, j, QXT[j, 0]))
    for k in range(1, 16):
        l32_copy(k).wait()
    prepare(3, lambda t, c: kv32[pl.ds(2 * c, 2), :, t].reshape(128, 128))
    for j in range(2):
        merge(j, 0, 128, *forward(3, j, QXT32[j]))

    wait_in(3)
    gather_order(3)
    for c in range(8):
        x = QG[c * 128:c * 128 + 128].astype(F32)
        xt = x.T
        for j in range(2):
            DOM[j, c * 128:c * 128 + 128] = jnp.where(half[j], x, 0.0).astype(BF16)
            DOT[j, c] = jnp.where(half_row[j], xt, 0.0).astype(BF16)

    def out_copy(t, k):
        return pltpu.make_async_remote_copy(
            src_ref=og.at[t, head_peer(k)], dst_ref=out_ref.at[t, h],
            send_sem=out_ss.at[t * 7 + k - 1], recv_sem=out_rs.at[t * 7 + k - 1],
            device_id={"head": head_peer(k)}, device_id_type=MESH)

    def out_local(t):
        return pltpu.make_async_copy(og.at[t, h], out_ref.at[t, h], loc_s.at[t])

    def start_out(t):
        for k in range(1, NH):
            out_copy(t, k).start()
        out_local(t).start()

    def scatter_order(t):
        og[t, :, 0:16] = QG[0:128].reshape(8, 16, 128)
        og[t, :, 16:64] = QG[128:512].reshape(8, 48, 128)
        og[t, :, 64:128] = QG[512:1024].reshape(8, 64, 128)

    for b in range(4):
        outs = []
        for j in range(2):
            total = ST[1, j, b]
            o = OT[j, b] / total
            outs.append(o)
            dot_up = wide(DOT, j, b)[64 * j:64 * j + 64].astype(F32)
            ST[0, j, b] = ST[0, j, b] + jnp.log(total)
            ST[1, j, b] = jnp.sum(dot_up * o, axis=0, keepdims=True)
        QG[b * 256:b * 256 + 256] = jnp.concatenate(outs, axis=0).T.astype(BF16)
    scatter_order(0)
    start_out(0)

    def backward(level, j, b, width, qxt, dot_t, rows):
        p = jnp.exp(nn(KX[level, j], qxt) - ST[0, j, b, :, :width])
        ACC[level, 1] += nn(p.astype(BF16), DOM[j, rows])
        dp = nn(VN[level], dot_t)
        ds = (p * (dp - ST[1, j, b, :, :width])).astype(BF16)
        ACC[level, 0] += nn(ds, QM[j, rows])
        return nn(KT[level, 64 * j:64 * j + 64], ds)

    DQT[...] = jnp.zeros(DQT.shape, F32)
    for j in range(2):
        DQT[j, 0, :, 0:128] += backward(3, j, 0, 128, QXT32[j], DOT[j, 0], pl.ds(0, 128))
    for t in range(2):
        g32[:, :, t] = ACC[3, t].reshape(16, 2, 32, 128).astype(BF16)

    def g32_copy(k):
        return pltpu.make_async_remote_copy(
            src_ref=g32.at[k], dst_ref=r32.at[16 - k],
            send_sem=l32_ss.at[14 + k], recv_sem=l32_rs.at[14 + k],
            device_id={"seq": plane_peer(k)}, device_id_type=MESH)

    for k in range(1, 16):
        g32_copy(k).start()

    for j in range(2):
        DQT[j, 0, :, 0:128] += backward(2, j, 0, 128, QXT[j, 0], DOT[j, 0], pl.ds(0, 128))
    for t in range(2):
        g8[:, t] = ACC[2, t].reshape(8, 128, 128).astype(BF16)

    def g8_copy(k):
        return pltpu.make_async_remote_copy(
            src_ref=g8.at[k], dst_ref=r8.at[8 - k],
            send_sem=l8_ss.at[6 + k], recv_sem=l8_rs.at[6 + k],
            device_id={"seq": oct_peer(k)}, device_id_type=MESH)

    for k in range(1, 8):
        g8_copy(k).start()

    def backward_level(level):
        def body(b, carry):
            for j in range(2):
                rows = pl.ds(pl.multiple_of(b * 256, 256), 256)
                DQT[j, b] += backward(level, j, b, 256, wide(QXT, j, b), wide(DOT, j, b), rows)
            return carry

        return body

    lax.fori_loop(0, 2, backward_level(1), 0)
    for t in range(2):
        g2[t] = ACC[1, t, 512:1024].reshape(8, 64, 128).astype(BF16)
    g2_copy = pltpu.make_async_remote_copy(
        src_ref=g2, dst_ref=r2, send_sem=l2_ss.at[1], recv_sem=l2_rs.at[1],
        device_id={"seq": pair}, device_id_type=MESH)
    g2_copy.start()

    for k in range(1, 16):
        g32_copy(k).wait()
    sum32 = []
    for t in range(2):
        mine, theirs = ACC[3, t, 0:32], ACC[3, t, 32:64]
        for m in range(1, 16):
            mine += r32[m, 0, t].astype(F32)
            theirs += r32[m, 1, t].astype(F32)
        ACC[3, t, 0:32] = mine
        g32z[t] = theirs.astype(BF16)
    gz_copy = pltpu.make_async_remote_copy(
        src_ref=g32z, dst_ref=r32z, send_sem=z_ss.at[1], recv_sem=z_rs.at[1],
        device_id={"seq": zpeer}, device_id_type=MESH)
    gz_copy.start()

    lax.fori_loop(0, 4, backward_level(0), 0)

    for b in range(4):
        both = jnp.concatenate([DQT[0, b], DQT[1, b]], axis=0) * 0.125
        QG[b * 256:b * 256 + 256] = both.T.astype(BF16)
    scatter_order(1)
    start_out(1)

    g2_copy.wait()
    for k in range(1, 8):
        g8_copy(k).wait()
    gz_copy.wait()
    put_row, put_col = iota((128, 32), 0), iota((128, 32), 1)
    put = (put_row == (put_col >> 2) * 16 + (put_col & 3)).astype(F32).astype(BF16)
    for t in range(2):
        acc1 = ACC.at[0, t]
        t8 = ACC[2, t, 0:128]
        for m in range(1, 8):
            t8 += r8[m, t].astype(F32)
        t32 = ACC[3, t, 0:32] + r32z[t].astype(F32)
        hi = t32.astype(BF16)
        lo = (t32 - hi.astype(F32)).astype(BF16)
        t8 = t8 + nn(put, hi) + nn(put, lo)
        for b in range(8):
            t2 = ACC[1, t, b * 64:b * 64 + 64] + r2[t, b].astype(F32)
            own = acc1[b * 128:b * 128 + 128]
            og[2 + t, b, 0:16] = (own[0:16] + t2[0:16] + t8[b * 16:b * 16 + 16]).astype(BF16)
            og[2 + t, b, 16:64] = (own[16:64] + t2[16:64]).astype(BF16)
            og[2 + t, b, 64:128] = own[64:128].astype(BF16)
        start_out(2 + t)

    for t in range(4):
        for k in range(1, NH):
            in_copy(t, k).wait_send()
    for t in range(4):
        for k in range(1, NH):
            out_copy(t, k).wait()
        out_local(t).wait()


def restore_kernel(packed_ref, a_ref, q_ref, k_ref, v_ref):
    low64 = iota((64, 128), 1) < 64
    outs = (a_ref, q_ref, k_ref, v_ref)
    for g in range(NH):
        rho = iota((NB, NB), 1)
        mat = (iota((NB, NB), 0) == token_of(rho >> 6, rho & 63, g)).astype(F32).astype(BF16)
        cols = []
        for t in range(4):
            first, second = packed_ref[t, g, 0:64].astype(F32), packed_ref[t, g, 64:128].astype(F32)
            cols.append(jnp.concatenate(
                [jnp.where(low64, first, second), jnp.where(low64, second, first)], axis=0).astype(BF16))
        res = nn(mat, jnp.concatenate(cols, axis=1))
        for t in range(4):
            outs[t][:, g * 128:g * 128 + 128] = res[:, t * 128:t * 128 + 128].astype(BF16)


def body(queries, keys, values, grad_out, doc_ids):
    vmem = pl.BlockSpec(memory_space=pltpu.VMEM)
    dma = pltpu.SemaphoreType.DMA
    packed = pl.pallas_call(
        attend_kernel,
        out_shape=jax.ShapeDtypeStruct((4, NH, NB, 128), BF16),
        in_specs=[vmem] * 5,
        out_specs=vmem,
        scratch_shapes=[
            pltpu.VMEM((4, NH, NB, 128), BF16),
            pltpu.VMEM((4, NH, NB, 128), BF16),
            pltpu.VMEM((2, 2, 8, 64, 128), BF16),
            pltpu.VMEM((8, 2, 8, 16, 128), BF16),
            pltpu.VMEM((16, 2, 2, 32, 128), BF16),
            pltpu.VMEM((4, 2, 1024, 128), BF16),
            pltpu.VMEM((4, 128, 1024), BF16),
            pltpu.VMEM((4, 128, 1024), BF16),
            pltpu.VMEM((4, 1024, 128), BF16),
            pltpu.VMEM((1024, 128), BF16),
            pltpu.VMEM((2, 8, 128, 128), BF16),
            pltpu.VMEM((2, 128, 128), BF16),
            pltpu.VMEM((2, 1024, 128), BF16),
            pltpu.VMEM((2, 1024, 128), BF16),
            pltpu.VMEM((2, 8, 128, 128), BF16),
            pltpu.VMEM((2, 2, 4, 1, 256), F32),
            pltpu.VMEM((2, 4, 64, 256), F32),
            pltpu.VMEM((2, 4, 64, 256), F32),
            pltpu.VMEM((4, 2, 1024, 128), F32),
            pltpu.VMEM((2, 8, 64, 128), BF16),
            pltpu.VMEM((2, 8, 64, 128), BF16),
            pltpu.VMEM((8, 2, 128, 128), BF16),
            pltpu.VMEM((8, 2, 128, 128), BF16),
            pltpu.VMEM((16, 2, 2, 32, 128), BF16),
            pltpu.VMEM((16, 2, 2, 32, 128), BF16),
            pltpu.VMEM((2, 32, 128), BF16),
            pltpu.VMEM((2, 32, 128), BF16),
            pltpu.VMEM((4, NH, NB, 128), BF16),
            dma((28,)), dma((28,)), dma((4,)),
            dma((2,)), dma((2,)), dma((14,)), dma((14,)), dma((30,)), dma((30,)),
            dma((2,)), dma((2,)), dma((28,)), dma((28,)),
        ],
        compiler_params=pltpu.CompilerParams(
            collective_id=0, has_side_effects=True, vmem_limit_bytes=56 * 1024 * 1024),
        name="attend",
    )(queries, keys, values, grad_out, doc_ids.reshape(256, 128))
    shape = jax.ShapeDtypeStruct(queries.shape, BF16)
    return pl.pallas_call(
        restore_kernel,
        out_shape=(shape, shape, shape, shape),
        in_specs=[vmem],
        out_specs=(vmem, vmem, vmem, vmem),
        compiler_params=pltpu.CompilerParams(vmem_limit_bytes=32 * 1024 * 1024),
        name="restore",
    )(packed)


def solution(mesh):
    spec = P(("seq", "head"), None)
    return jax.shard_map(
        body, mesh=mesh, in_specs=(spec, spec, spec, spec, P()), out_specs=(spec, spec, spec, spec), check_vma=False)
```

```python
import jax
import jax.numpy as jnp
from jax import lax
from jax.experimental import pallas as pl
from jax.experimental.pallas import tpu as pltpu
from jax.sharding import PartitionSpec as P

F32 = jnp.float32
BF16 = jnp.bfloat16
I32 = jnp.int32
BIG = 1e30
NH = 8
NB = 128
MESH = pl.DeviceIdType.MESH
ROW_O, ROW_Q, ROW_KV, ROW_T8, ROW_TZ, ROWS = (0, 64), (128, 192), (256, 384), (512, 528), (544, 560), 576


def iota(shape, dim):
    return lax.broadcasted_iota(I32, shape, dim)


def token_of(parity, w, h):
    t, u, a = (w >> 4) & 3, (w >> 2) & 3, w & 3
    return a * 32 + parity + 2 * ((h + t) & 3) + 8 * ((h // 4 + u) & 3)


def nn(a, b):
    return lax.dot_general(a, b, (((1,), (0,)), ((), ())), preferred_element_type=F32)


def attend_kernel(
    q_hbm, k_hbm, v_hbm, do_hbm, docs_hbm, out_ref,
    q_ref, k_ref, v_ref, do_ref, docs_ref,
    send, inbuf, zin, kv2, kv8, kv32, KX, KVT, QG, QXT, QXT32, QM, DOM, DOT,
    ST, OT, DQT, ACC, g2, r2, g8, r8, g32, r32, og,
    load_s, in_ss, in_rs, zin_ss, zin_rs, loc_s, l2_ss, l2_rs, l8_ss, l8_rs, l32_ss, l32_rs,
    out_ss, out_rs, tz_ss, tz_rs, out_loc,
):
    h = lax.axis_index("head")
    s = lax.axis_index("seq")
    pair = s + 1 - 2 * (s % 2)
    base8 = (s // 8) * 8
    base16 = (s // 16) * 16
    zpeer = (s + 16) % 32

    def plane_peer(k):
        return base16 + (s - base16 + k) % 16

    def oct_peer(k):
        return base8 + (s - base8 + k) % 8

    def head_peer(k):
        return (h + k) % NH

    barrier = pltpu.get_barrier_semaphore()
    for k in range(1, NH):
        pl.semaphore_signal(barrier, inc=1, device_id={"head": head_peer(k)}, device_id_type=MESH)
    for k in range(1, 16):
        pl.semaphore_signal(barrier, inc=1, device_id={"seq": plane_peer(k)}, device_id_type=MESH)
    for k in range(NH):
        pl.semaphore_signal(barrier, inc=1, device_id={"seq": zpeer, "head": head_peer(k)}, device_id_type=MESH)

    pairs = ((k_hbm, k_ref), (v_hbm, v_ref), (q_hbm, q_ref), (do_hbm, do_ref), (docs_hbm, docs_ref))
    loads = [pltpu.make_async_copy(a, b, load_s.at[i]) for i, (a, b) in enumerate(pairs)]
    for load in loads:
        load.start()

    lane128 = iota((128, 128), 1)
    row128 = iota((128, 128), 0)
    low = lane128 < 64

    def permute_two(first, a_ref, b_ref):
        for g in range(NH):
            mat = (lane128 == token_of(row128 >> 6, row128 & 63, g)).astype(F32).astype(BF16)
            cols = slice(g * 128, g * 128 + 128)
            res = nn(mat, jnp.concatenate([a_ref[:, cols], b_ref[:, cols]], axis=1))
            a, b = res[:, 0:128], res[:, 128:256]
            send[first, g] = jnp.where(low, a, pltpu.roll(b, 64, 1)).astype(BF16)
            other = jnp.where(low, pltpu.roll(a, 64, 1), b).astype(BF16)
            send[first + 2, g, 0:64] = other[64:128]
            send[first + 2, g, 64:128] = other[0:64]

    def in_copy(t, k):
        return pltpu.make_async_remote_copy(
            src_ref=send.at[t, head_peer(k)], dst_ref=inbuf.at[t, h],
            send_sem=in_ss.at[t * 7 + k - 1], recv_sem=in_rs.at[t * 7 + k - 1],
            device_id={"head": head_peer(k)}, device_id_type=MESH)

    def in_local(t):
        return pltpu.make_async_copy(send.at[t, h], inbuf.at[t, h], loc_s.at[t])

    def start_in(t):
        for k in range(1, NH):
            in_copy(t, k).start()
        in_local(t).start()

    def wait_in(t):
        for k in range(1, NH):
            in_copy(t, k).wait_recv()
        in_local(t).wait()

    def zin_copy(j, k):
        return pltpu.make_async_remote_copy(
            src_ref=send.at[2 * j, head_peer(k), pl.ds(0, 16)], dst_ref=zin.at[j, h],
            send_sem=zin_ss.at[8 * j + k], recv_sem=zin_rs.at[8 * j + k],
            device_id={"seq": zpeer, "head": head_peer(k)}, device_id_type=MESH)

    def start_keys(j):
        for k in range(NH):
            zin_copy(j, k).start()
        start_in(2 * j)

    loads[0].wait()
    loads[1].wait()
    permute_two(0, k_ref, v_ref)
    loads[2].wait()
    loads[3].wait()
    permute_two(1, q_ref, do_ref)
    pl.semaphore_wait(barrier, 30)
    start_keys(0)
    start_in(1)
    loads[4].wait()

    docs = docs_ref[...]

    def count(limit):
        c = jnp.sum((docs < limit).astype(F32), axis=0, keepdims=True)
        return jnp.sum(c, axis=1, keepdims=True).astype(I32)

    bound1, bound2 = count(1), count(2)

    def doc_of(pos):
        return (pos >= bound1).astype(I32) + (pos >= bound2).astype(I32)

    def key_place(level, c):
        r = row128 + c * 128
        if level == 0:
            return s, r >> 7, r & 127
        if level == 1:
            return jnp.where((r >> 9) == 0, s, pair), (r >> 6) & 7, r & 63
        if level == 2:
            return base8 + ((s + (r >> 7)) & 7), (r >> 4) & 7, r & 15
        plane = jnp.where(((r >> 5) & 1) == 0, base16, 16 - base16)
        return plane + ((s + (r >> 6)) & 15), (r >> 2) & 7, r & 3

    def fill_features(c, carry):
        for level in range(4):
            seqs, src, w = key_place(level, c)
            start = seqs * 1024 + src * 128
            for j in range(2):
                parity = j ^ (w >> 6)
                doc = doc_of(start + token_of(parity, w & 63, h))
                hot = (lane128 - 64 == doc) | (lane128 == 67)
                KX[level, j, pl.ds(c * 128, 128)] = jnp.where(hot, 1.0, 0.0).astype(BF16)
        return carry

    lax.fori_loop(0, 8, fill_features, 0)

    feat_row = row128 - 64
    for c in range(8):
        if c % 4 == 0:
            src, w = lane128 >> 4, lane128 & 15
        else:
            i = lane128 + (c % 4 - 1) * 128
            src = (i * 1366) >> 16
            w = 16 + i - src * 48
        w = w + 64 * (c // 4)
        for j in range(2):
            parity = j ^ (w >> 6)
            doc = doc_of(s * 1024 + src * 128 + token_of(parity, w & 63, h))
            hide = (feat_row >= 0) & (feat_row < 3) & (feat_row != doc)
            QXT[j, c] = jnp.where(hide, -BIG, 0.0).astype(BF16)
            if c == 0:
                hide = hide | ((feat_row == 3) & (w >= 4))
                QXT32[j] = jnp.where(hide, -BIG, 0.0).astype(BF16)

    ACC[...] = jnp.zeros(ACC.shape, F32)
    DQT[...] = jnp.zeros(DQT.shape, F32)

    def l2_copy(j):
        return pltpu.make_async_remote_copy(
            src_ref=inbuf.at[2 * j, :, pl.ds(0, 64), :], dst_ref=kv2.at[j, 1],
            send_sem=l2_ss.at[j], recv_sem=l2_rs.at[j], device_id={"seq": pair}, device_id_type=MESH)

    def l8_copy(j, k):
        return pltpu.make_async_remote_copy(
            src_ref=inbuf.at[2 * j, :, pl.ds(0, 16), :], dst_ref=kv8.at[j, 8 - k],
            send_sem=l8_ss.at[7 * j + k - 1], recv_sem=l8_rs.at[7 * j + k - 1],
            device_id={"seq": oct_peer(k)}, device_id_type=MESH)

    def l32_copy(j, k):
        return pltpu.make_async_remote_copy(
            src_ref=kv32.at[j, 0], dst_ref=kv32.at[j, 16 - k],
            send_sem=l32_ss.at[15 * j + k - 1], recv_sem=l32_rs.at[15 * j + k - 1],
            device_id={"seq": plane_peer(k)}, device_id_type=MESH)

    pick_row, pick_col = iota((32, 128), 0), iota((32, 128), 1)
    pick = (pick_col == (pick_row >> 2) * 16 + (pick_row & 3)).astype(F32).astype(BF16)

    def start_levels(j):
        l2_copy(j).start()
        for k in range(1, 8):
            l8_copy(j, k).start()
        for k in range(NH):
            zin_copy(j, k).wait_recv()
        kv32[j, 0, 0] = nn(pick, inbuf[2 * j, :, 0:16].reshape(128, 128)).astype(BF16)
        kv32[j, 0, 1] = nn(pick, zin[j].reshape(128, 128)).astype(BF16)
        for k in range(1, 16):
            l32_copy(j, k).start()
        kv2[j, 0] = inbuf[2 * j, :, 0:64]
        kv8[j, 0] = inbuf[2 * j, :, 0:16]

    def prepare(level, j, load):
        def chunk(c, carry):
            rows = pl.ds(pl.multiple_of(c * 128, 128), 128)
            kv = load(c).astype(F32)
            KX[level, j, rows] = jnp.where(low, kv, KX[level, j, rows].astype(F32)).astype(BF16)
            KVT[level, j, :, rows] = kv.T.astype(BF16)
            return carry

        lax.fori_loop(0, 8, chunk, 0)

    def natural(level, j):
        ref = (inbuf.at[2 * j], kv2.at[j], kv8.at[j], kv32.at[j])[level]
        return ref[...].reshape(1024, 128)

    def prepare_queries(j):
        x = inbuf.at[2 * j + 1]
        QG[0:128] = x[:, 0:16].reshape(128, 128)
        QG[128:512] = x[:, 16:64].reshape(384, 128)
        QG[512:640] = x[:, 64:80].reshape(128, 128)
        QG[640:1024] = x[:, 80:128].reshape(384, 128)
        for c in range(8):
            rows = slice(c * 128, c * 128 + 128)
            qd = QG[rows].astype(F32)
            query, up = qd * 0.125, jnp.where(low, 0.0, qd)
            query_t = query.T
            QM[j, rows] = jnp.where(low, query, 0.0).astype(BF16)
            DOM[j, rows] = up.astype(BF16)
            DOT[j, c] = up.T.astype(BF16)
            QXT[j, c] = jnp.where(row128 < 64, query_t, QXT[j, c].astype(F32)).astype(BF16)
            if c == 0:
                QXT32[j] = jnp.where(row128 < 64, query_t, QXT32[j].astype(F32)).astype(BF16)

    def wide(ref, j, b):
        return jnp.concatenate([ref[j, 4 * b + i] for i in range(4)], axis=1)

    def forward(level, j, qxt):
        sc = nn(KX[level, j], qxt)
        m = jnp.max(sc, axis=0, keepdims=True)
        w = jnp.exp(sc - m)
        total = jnp.sum(w, axis=0, keepdims=True)
        o = nn(KVT[level, j, 64:128], w.astype(BF16))
        return m, total, o

    def merge(j, b, width, m, total, o):
        m0, l0, o0 = ST[0, j, b, :, :width], ST[1, j, b, :, :width], OT[j, b, :, :width]
        mm = jnp.maximum(m0, m)
        e0, e1 = jnp.exp(m0 - mm), jnp.exp(m - mm)
        ST[0, j, b, :, :width] = mm
        ST[1, j, b, :, :width] = l0 * e0 + total * e1
        OT[j, b, :, :width] = o0 * e0 + o * e1

    def forward_first(j):
        def step(i, carry):
            m, total, o = forward(0, j, wide(QXT, j, i))
            ST[0, j, i] = m
            ST[1, j, i] = total
            OT[j, i] = o
            return carry

        lax.fori_loop(0, 2, step, 0)

    def forward_rest(j):
        l2_copy(j).wait()
        prepare(1, j, lambda c: kv2[j, c // 4, pl.ds((c % 4) * 2, 2)].reshape(128, 128))
        merge(j, 0, 512, *forward(1, j, wide(QXT, j, 0)))
        for k in range(1, 8):
            l8_copy(j, k).wait()
        prepare(2, j, lambda c: kv8[j, c].reshape(128, 128))
        merge(j, 0, 128, *forward(2, j, QXT[j, 0]))
        for k in range(1, 16):
            l32_copy(j, k).wait()
        prepare(3, j, lambda c: kv32[j, pl.ds(2 * c, 2)].reshape(128, 128))
        merge(j, 0, 128, *forward(3, j, QXT32[j]))
        for b in range(2):
            total = ST[1, j, b]
            o = OT[j, b] / total
            OT[j, b] = o
            ST[0, j, b] = ST[0, j, b] + jnp.log(total)
            ST[1, j, b] = jnp.sum(wide(DOT, j, b)[64:128].astype(F32) * o, axis=0, keepdims=True)

    def out_copy(i, src, row, n, k):
        return pltpu.make_async_remote_copy(
            src_ref=src.at[head_peer(k)], dst_ref=out_ref.at[h, pl.ds(row, n)],
            send_sem=out_ss.at[i * 7 + k - 1], recv_sem=out_rs.at[i * 7 + k - 1],
            device_id={"head": head_peer(k)}, device_id_type=MESH)

    def out_local(i, src, row, n):
        return pltpu.make_async_copy(src.at[h], out_ref.at[h, pl.ds(row, n)], out_loc.at[i])

    def og_part(row, n):
        return og.at[:, pl.ds(row, n)]

    parts = []
    for j in range(2):
        parts += [(ROW_O[j], 64), (ROW_Q[j], 64), (ROW_KV[j], 128), (ROW_T8[j], 16)]

    def start_out(i):
        row, n = parts[i]
        for k in range(1, NH):
            out_copy(i, og_part(row, n), row, n, k).start()
        out_local(i, og_part(row, n), row, n).start()

    def tz_copy(j, k):
        return pltpu.make_async_remote_copy(
            src_ref=og.at[head_peer(k), pl.ds(ROW_TZ[j], 16)], dst_ref=out_ref.at[h, pl.ds(ROW_TZ[j], 16)],
            send_sem=tz_ss.at[8 * j + k], recv_sem=tz_rs.at[8 * j + k],
            device_id={"seq": zpeer, "head": head_peer(k)}, device_id_type=MESH)

    def send_rows(i, top, bottom):
        row = parts[i][0]
        both = jnp.concatenate([top, bottom], axis=0).T.astype(BF16)
        og[:, row:row + 16] = both[0:128].reshape(8, 16, 128)
        og[:, row + 16:row + 64] = both[128:512].reshape(8, 48, 128)
        start_out(i)

    def backward(level, j, b, width, qxt, dot_t, rows):
        p = jnp.exp(nn(KX[level, j], qxt) - ST[0, j, b, :, :width])
        dp = nn(natural(level, j), dot_t)
        ds = (p * (dp - ST[1, j, b, :, :width])).astype(BF16)
        ACC[level, j] += nn(ds, QM[j, rows]) + nn(p.astype(BF16), DOM[j, rows])
        DQT[j, b, :, :width] += nn(KVT[level, j, 0:64], ds)

    def g32_copy(j, k):
        return pltpu.make_async_remote_copy(
            src_ref=g32.at[j, k], dst_ref=r32.at[j, 16 - k],
            send_sem=l32_ss.at[29 + 15 * j + k], recv_sem=l32_rs.at[29 + 15 * j + k],
            device_id={"seq": plane_peer(k)}, device_id_type=MESH)

    def g8_copy(j, k):
        return pltpu.make_async_remote_copy(
            src_ref=g8.at[j, k], dst_ref=r8.at[j, 8 - k],
            send_sem=l8_ss.at[13 + 7 * j + k], recv_sem=l8_rs.at[13 + 7 * j + k],
            device_id={"seq": oct_peer(k)}, device_id_type=MESH)

    def g2_copy(j):
        return pltpu.make_async_remote_copy(
            src_ref=g2.at[j], dst_ref=r2.at[j], send_sem=l2_ss.at[2 + j], recv_sem=l2_rs.at[2 + j],
            device_id={"seq": pair}, device_id_type=MESH)

    def backward_sparse(j):
        backward(3, j, 0, 128, QXT32[j], DOT[j, 0], pl.ds(0, 128))
        g32[j] = ACC[3, j].reshape(16, 2, 32, 128).astype(BF16)
        for k in range(1, 16):
            g32_copy(j, k).start()
        backward(2, j, 0, 128, QXT[j, 0], DOT[j, 0], pl.ds(0, 128))
        g8[j] = ACC[2, j].reshape(8, 128, 128).astype(BF16)
        for k in range(1, 8):
            g8_copy(j, k).start()

    def backward_pair(j):
        backward(1, j, 0, 512, wide(QXT, j, 0), wide(DOT, j, 0), pl.ds(0, 512))
        g2[j] = ACC[1, j, 512:1024].reshape(8, 64, 128).astype(BF16)
        g2_copy(j).start()

    def backward_local(j):
        def step(i, carry):
            rows = pl.ds(pl.multiple_of(i * 512, 512), 512)
            backward(0, j, i, 512, wide(QXT, j, i), wide(DOT, j, i), rows)
            return carry

        lax.fori_loop(0, 2, step, 0)

    put_row, put_col = iota((128, 32), 0), iota((128, 32), 1)
    put = (put_row == (put_col >> 2) * 16 + (put_col & 3)).astype(F32).astype(BF16)

    def send_keys(j):
        g2_copy(j).wait()
        for b in range(8):
            t2 = ACC[1, j, b * 64:b * 64 + 64] + r2[j, b].astype(F32)
            own = ACC[0, j, b * 128:b * 128 + 128]
            og[b, ROW_KV[j]:ROW_KV[j] + 64] = (own[0:64] + t2).astype(BF16)
            og[b, ROW_KV[j] + 64:ROW_KV[j] + 128] = own[64:128].astype(BF16)
        start_out(4 * j + 2)

    def spread(x):
        hi = x.astype(BF16)
        return nn(put, hi) + nn(put, (x - hi.astype(F32)).astype(BF16))

    def send_tiles(j):
        for k in range(1, 16):
            g32_copy(j, k).wait()
        mine, theirs = ACC[3, j, 0:32], ACC[3, j, 32:64]
        for m in range(1, 16):
            mine += r32[j, m, 0].astype(F32)
            theirs += r32[j, m, 1].astype(F32)
        og[:, ROW_TZ[j]:ROW_TZ[j] + 16] = spread(theirs).astype(BF16).reshape(8, 16, 128)
        for k in range(NH):
            tz_copy(j, k).start()
        for k in range(1, 8):
            g8_copy(j, k).wait()
        t8 = ACC[2, j, 0:128] + spread(mine)
        for m in range(1, 8):
            t8 += r8[j, m].astype(F32)
        og[:, ROW_T8[j]:ROW_T8[j] + 16] = t8.astype(BF16).reshape(8, 16, 128)
        start_out(4 * j + 3)

    def prepare_local(j):
        prepare(0, j, lambda c: inbuf[2 * j, c])

    def send_output(j):
        send_rows(4 * j, OT[j, 0], OT[j, 1])

    def send_queries(j):
        send_rows(4 * j + 1, DQT[j, 0] * 0.125, DQT[j, 1] * 0.125)

    wait_in(0)
    start_keys(1)
    start_levels(0)
    prepare_local(0)
    wait_in(1)
    start_in(3)
    prepare_queries(0)
    forward_first(0)
    forward_rest(0)
    send_output(0)
    wait_in(2)
    start_levels(1)
    backward_pair(0)
    backward_sparse(0)
    prepare_local(1)
    backward_local(0)
    send_queries(0)
    wait_in(3)
    prepare_queries(1)
    forward_first(1)
    send_keys(0)
    send_tiles(0)
    forward_rest(1)
    send_output(1)
    backward_pair(1)
    backward_sparse(1)
    backward_local(1)
    send_queries(1)
    send_keys(1)
    send_tiles(1)

    for t in range(4):
        for k in range(1, NH):
            in_copy(t, k).wait_send()
    for j in range(2):
        for k in range(NH):
            zin_copy(j, k).wait_send()
            tz_copy(j, k).wait()
    for i, (row, n) in enumerate(parts):
        for k in range(1, NH):
            out_copy(i, og_part(row, n), row, n, k).wait()
        out_local(i, og_part(row, n), row, n).wait()


def restore_kernel(packed_ref, a_ref, q_ref, k_ref, v_ref):
    low = iota((128, 128), 1) < 64
    low64 = iota((64, 128), 1) < 64
    for g in range(NH):
        rho = iota((NB, NB), 1)
        mat = (iota((NB, NB), 0) == token_of(rho >> 6, rho & 63, g)).astype(F32).astype(BF16)
        cols = []
        for rows in (ROW_O, ROW_Q):
            x, y = (packed_ref[g, row:row + 64].astype(F32) for row in rows)
            odd = pltpu.roll(jnp.where(low64, y, x), 64, 1)
            cols.append(jnp.concatenate([jnp.where(low64, x, y), odd], axis=0).astype(BF16))
        for j in range(2):
            tile = sum(packed_ref[g, row:row + 16].astype(F32) for row in (ROW_KV[j], ROW_T8[j], ROW_TZ[j]))
            own = [tile.astype(BF16), packed_ref[g, ROW_KV[j] + 16:ROW_KV[j] + 64]]
            other = [packed_ref[g, ROW_KV[j] + 64:ROW_KV[j] + 128]]
            cols.append(jnp.concatenate(other + own if j else own + other, axis=0))
        res = nn(mat, jnp.concatenate(cols, axis=1))
        here = slice(g * 128, g * 128 + 128)
        a_ref[:, here] = res[:, 0:128].astype(BF16)
        q_ref[:, here] = res[:, 128:256].astype(BF16)
        x, y = res[:, 256:384], res[:, 384:512]
        k_ref[:, here] = jnp.where(low, x, pltpu.roll(y, 64, 1)).astype(BF16)
        v_ref[:, here] = jnp.where(low, pltpu.roll(x, 64, 1), y).astype(BF16)


def body(queries, keys, values, grad_out, doc_ids):
    vmem = pl.BlockSpec(memory_space=pltpu.VMEM)
    dma = pltpu.SemaphoreType.DMA
    packed = pl.pallas_call(
        attend_kernel,
        out_shape=jax.ShapeDtypeStruct((NH, ROWS, 128), BF16),
        in_specs=[pl.BlockSpec(memory_space=pl.ANY)] * 5,
        out_specs=pl.BlockSpec(memory_space=pl.ANY),
        scratch_shapes=[pltpu.VMEM(queries.shape, BF16)] * 4 + [
            pltpu.VMEM((256, 128), I32),
            pltpu.VMEM((4, NH, NB, 128), BF16),
            pltpu.VMEM((4, NH, NB, 128), BF16),
            pltpu.VMEM((2, 8, 16, 128), BF16),
            pltpu.VMEM((2, 2, 8, 64, 128), BF16),
            pltpu.VMEM((2, 8, 8, 16, 128), BF16),
            pltpu.VMEM((2, 16, 2, 32, 128), BF16),
            pltpu.VMEM((4, 2, 1024, 128), BF16),
            pltpu.VMEM((4, 2, 128, 1024), BF16),
            pltpu.VMEM((1024, 128), BF16),
            pltpu.VMEM((2, 8, 128, 128), BF16),
            pltpu.VMEM((2, 128, 128), BF16),
            pltpu.VMEM((2, 1024, 128), BF16),
            pltpu.VMEM((2, 1024, 128), BF16),
            pltpu.VMEM((2, 8, 128, 128), BF16),
            pltpu.VMEM((2, 2, 2, 1, 512), F32),
            pltpu.VMEM((2, 2, 64, 512), F32),
            pltpu.VMEM((2, 2, 64, 512), F32),
            pltpu.VMEM((4, 2, 1024, 128), F32),
            pltpu.VMEM((2, 8, 64, 128), BF16),
            pltpu.VMEM((2, 8, 64, 128), BF16),
            pltpu.VMEM((2, 8, 128, 128), BF16),
            pltpu.VMEM((2, 8, 128, 128), BF16),
            pltpu.VMEM((2, 16, 2, 32, 128), BF16),
            pltpu.VMEM((2, 16, 2, 32, 128), BF16),
            pltpu.VMEM((NH, ROWS, 128), BF16),
            dma((5,)), dma((28,)), dma((28,)), dma((16,)), dma((16,)), dma((4,)),
            dma((4,)), dma((4,)), dma((28,)), dma((28,)), dma((60,)), dma((60,)),
            dma((56,)), dma((56,)), dma((16,)), dma((16,)), dma((8,)),
        ],
        compiler_params=pltpu.CompilerParams(
            collective_id=0, has_side_effects=True, vmem_limit_bytes=56 * 1024 * 1024),
        name="attend",
    )(queries, keys, values, grad_out, doc_ids.reshape(256, 128))
    shape = jax.ShapeDtypeStruct(queries.shape, BF16)
    return pl.pallas_call(
        restore_kernel,
        out_shape=(shape, shape, shape, shape),
        in_specs=[vmem],
        out_specs=(vmem, vmem, vmem, vmem),
        compiler_params=pltpu.CompilerParams(vmem_limit_bytes=32 * 1024 * 1024),
        name="restore",
    )(packed)


def solution(mesh):
    spec = P(("seq", "head"), None)
    return jax.shard_map(
        body, mesh=mesh, in_specs=(spec, spec, spec, spec, P()), out_specs=(spec, spec, spec, spec), check_vma=False)
```

```python
import jax
import jax.numpy as jnp
from jax import lax
from jax.experimental import pallas as pl
from jax.experimental.pallas import tpu as pltpu
from jax.sharding import PartitionSpec as P

F32 = jnp.float32
BF16 = jnp.bfloat16
I32 = jnp.int32
BIG = 1e30
NH = 8
NB = 128
MESH = pl.DeviceIdType.MESH
ROW_Q, ROW_KV, ROW_T8, ROW_TZ, ROWS = ((0, 64), (128, 192)), (256, 384), (512, 528), (544, 560), 576


def iota(shape, dim):
    return lax.broadcasted_iota(I32, shape, dim)


def token_of(parity, w, h):
    t, u, a = (w >> 4) & 3, (w >> 2) & 3, w & 3
    return a * 32 + parity + 2 * ((h + t) & 3) + 8 * ((h // 4 + u) & 3)


def nn(a, b):
    return lax.dot_general(a, b, (((1,), (0,)), ((), ())), preferred_element_type=F32)


def attend_kernel(
    q_hbm, k_hbm, v_hbm, do_hbm, docs_hbm, out_ref,
    q_ref, k_ref, v_ref, do_ref, docs_ref,
    send, inbuf, zin, kv2, kv8, kv32, KX, KVT, QG, QXT, QXT32, QM, DOM, DOT,
    W1, W2, W8, W32, ACC, g2, r2, g8, r8, g32, r32, og,
    load_s, in_ss, in_rs, zin_ss, zin_rs, loc_s, l2_ss, l2_rs, l8_ss, l8_rs, l32_ss, l32_rs,
    out_ss, out_rs, tz_ss, tz_rs, out_loc,
):
    h = lax.axis_index("head")
    s = lax.axis_index("seq")
    pair = s + 1 - 2 * (s % 2)
    base8 = (s // 8) * 8
    base16 = (s // 16) * 16
    zpeer = (s + 16) % 32

    def plane_peer(k):
        return base16 + (s - base16 + k) % 16

    def oct_peer(k):
        return base8 + (s - base8 + k) % 8

    def head_peer(k):
        return (h + k) % NH

    barrier = pltpu.get_barrier_semaphore()
    for k in range(1, NH):
        pl.semaphore_signal(barrier, inc=1, device_id={"head": head_peer(k)}, device_id_type=MESH)
    for k in range(1, 16):
        pl.semaphore_signal(barrier, inc=1, device_id={"seq": plane_peer(k)}, device_id_type=MESH)
    for k in range(NH):
        pl.semaphore_signal(barrier, inc=1, device_id={"seq": zpeer, "head": head_peer(k)}, device_id_type=MESH)

    pairs = ((k_hbm, k_ref), (v_hbm, v_ref), (q_hbm, q_ref), (do_hbm, do_ref), (docs_hbm, docs_ref))
    loads = [pltpu.make_async_copy(a, b, load_s.at[i]) for i, (a, b) in enumerate(pairs)]
    for load in loads:
        load.start()

    lane128 = iota((128, 128), 1)
    row128 = iota((128, 128), 0)
    low = lane128 < 64

    def permute_two(first, a_ref, b_ref):
        for g in range(NH):
            mat = (lane128 == token_of(row128 >> 6, row128 & 63, g)).astype(F32).astype(BF16)
            cols = slice(g * 128, g * 128 + 128)
            res = nn(mat, jnp.concatenate([a_ref[:, cols], b_ref[:, cols]], axis=1))
            a, b = res[:, 0:128], res[:, 128:256]
            send[first, g] = jnp.where(low, a, pltpu.roll(b, 64, 1)).astype(BF16)
            other = jnp.where(low, pltpu.roll(a, 64, 1), b).astype(BF16)
            send[first + 2, g, 0:64] = other[64:128]
            send[first + 2, g, 64:128] = other[0:64]

    messages = ((0, 0, 128), (1, 64, 64), (2, 0, 128), (1, 0, 64), (3, 0, 64), (3, 64, 64))

    def in_copy(i, k):
        t, row, n = messages[i]
        return pltpu.make_async_remote_copy(
            src_ref=send.at[t, head_peer(k), pl.ds(row, n)], dst_ref=inbuf.at[t, h, pl.ds(row, n)],
            send_sem=in_ss.at[i * 7 + k - 1], recv_sem=in_rs.at[i * 7 + k - 1],
            device_id={"head": head_peer(k)}, device_id_type=MESH)

    def in_local(i):
        t, row, n = messages[i]
        return pltpu.make_async_copy(
            send.at[t, h, pl.ds(row, n)], inbuf.at[t, h, pl.ds(row, n)], loc_s.at[i])

    def start_in(i):
        for k in range(1, NH):
            in_copy(i, k).start()
        in_local(i).start()

    def wait_in(i):
        for k in range(1, NH):
            in_copy(i, k).wait_recv()
        in_local(i).wait()

    def zin_copy(j, k):
        return pltpu.make_async_remote_copy(
            src_ref=send.at[2 * j, head_peer(k), pl.ds(0, 16)], dst_ref=zin.at[j, h],
            send_sem=zin_ss.at[8 * j + k], recv_sem=zin_rs.at[8 * j + k],
            device_id={"seq": zpeer, "head": head_peer(k)}, device_id_type=MESH)

    def start_zin(j):
        for k in range(NH):
            zin_copy(j, k).start()

    loads[0].wait()
    loads[1].wait()
    permute_two(0, k_ref, v_ref)
    pl.semaphore_wait(barrier, 30)
    start_zin(0)
    start_in(0)
    loads[2].wait()
    loads[3].wait()
    permute_two(1, q_ref, do_ref)
    start_in(1)
    start_zin(1)
    for i in range(2, 6):
        start_in(i)
    loads[4].wait()

    docs = docs_ref[...]

    def count(limit):
        c = jnp.sum((docs < limit).astype(F32), axis=0, keepdims=True)
        return jnp.sum(c, axis=1, keepdims=True).astype(I32)

    bound1, bound2 = count(1), count(2)

    def doc_of(pos):
        return (pos >= bound1).astype(I32) + (pos >= bound2).astype(I32)

    def key_place(level, c):
        r = row128 + c * 128
        if level == 0:
            return s, r >> 7, r & 127
        if level == 1:
            return jnp.where((r >> 9) == 0, s, pair), (r >> 6) & 7, r & 63
        if level == 2:
            return base8 + ((s + (r >> 7)) & 7), (r >> 4) & 7, r & 15
        plane = jnp.where(((r >> 5) & 1) == 0, base16, 16 - base16)
        return plane + ((s + (r >> 6)) & 15), (r >> 2) & 7, r & 3

    def fill_features(c, carry):
        for level in range(4):
            seqs, src, w = key_place(level, c)
            start = seqs * 1024 + src * 128
            for j in range(2):
                parity = j ^ (w >> 6)
                doc = doc_of(start + token_of(parity, w & 63, h))
                hot = (lane128 - 64 == doc) | (lane128 == 67)
                KX[level, j, pl.ds(c * 128, 128)] = jnp.where(hot, 1.0, 0.0).astype(BF16)
        return carry

    lax.fori_loop(0, 8, fill_features, 0)

    feat_row = row128 - 64
    for c in range(8):
        if c % 4 == 0:
            src, w = lane128 >> 4, lane128 & 15
        else:
            i = lane128 + (c % 4 - 1) * 128
            src = (i * 1366) >> 16
            w = 16 + i - src * 48
        w = w + 64 * (c // 4)
        for j in range(2):
            parity = j ^ (w >> 6)
            doc = doc_of(s * 1024 + src * 128 + token_of(parity, w & 63, h))
            hide = (feat_row >= 0) & (feat_row < 3) & (feat_row != doc)
            QXT[j, c] = jnp.where(hide, -BIG, 0.0).astype(BF16)
            if c == 0:
                hide = hide | ((feat_row == 3) & (w >= 4))
                QXT32[j] = jnp.where(hide, -BIG, 0.0).astype(BF16)

    def l2_copy(j):
        return pltpu.make_async_remote_copy(
            src_ref=inbuf.at[2 * j, :, pl.ds(0, 64), :], dst_ref=kv2.at[j, 1],
            send_sem=l2_ss.at[j], recv_sem=l2_rs.at[j], device_id={"seq": pair}, device_id_type=MESH)

    def l8_copy(j, k):
        return pltpu.make_async_remote_copy(
            src_ref=inbuf.at[2 * j, :, pl.ds(0, 16), :], dst_ref=kv8.at[j, 8 - k],
            send_sem=l8_ss.at[7 * j + k - 1], recv_sem=l8_rs.at[7 * j + k - 1],
            device_id={"seq": oct_peer(k)}, device_id_type=MESH)

    def l32_copy(j, k):
        return pltpu.make_async_remote_copy(
            src_ref=kv32.at[j, 0], dst_ref=kv32.at[j, 16 - k],
            send_sem=l32_ss.at[15 * j + k - 1], recv_sem=l32_rs.at[15 * j + k - 1],
            device_id={"seq": plane_peer(k)}, device_id_type=MESH)

    pick_row, pick_col = iota((32, 128), 0), iota((32, 128), 1)
    pick = (pick_col == (pick_row >> 2) * 16 + (pick_row & 3)).astype(F32).astype(BF16)

    def start_levels(j):
        l2_copy(j).start()
        for k in range(1, 8):
            l8_copy(j, k).start()
        for k in range(NH):
            zin_copy(j, k).wait_recv()
        kv32[j, 0, 0] = nn(pick, inbuf[2 * j, :, 0:16].reshape(128, 128)).astype(BF16)
        kv32[j, 0, 1] = nn(pick, zin[j].reshape(128, 128)).astype(BF16)
        for k in range(1, 16):
            l32_copy(j, k).start()
        kv2[j, 0] = inbuf[2 * j, :, 0:64]
        kv8[j, 0] = inbuf[2 * j, :, 0:16]

    def prepare(level, j, load):
        def chunk(c, carry):
            rows = pl.ds(pl.multiple_of(c * 128, 128), 128)
            kv = load(c).astype(F32)
            KX[level, j, rows] = jnp.where(low, kv, KX[level, j, rows].astype(F32)).astype(BF16)
            KVT[level, j, :, rows] = kv.T.astype(BF16)
            return carry

        lax.fori_loop(0, 8, chunk, 0)

    def natural(level, j):
        ref = (inbuf.at[2 * j], kv2.at[j], kv8.at[j], kv32.at[j])[level]
        return ref[...].reshape(1024, 128)

    def prepare_queries(j, part):
        x = inbuf.at[2 * j + 1, :, pl.ds(64 * part, 64)]
        QG[0:128] = x[:, 0:16].reshape(128, 128)
        QG[128:512] = x[:, 16:64].reshape(384, 128)
        for i in range(4):
            c = 4 * part + i
            rows = slice(c * 128, c * 128 + 128)
            qd = QG[i * 128:i * 128 + 128].astype(F32)
            query, up = qd * 0.125, jnp.where(low, 0.0, qd)
            query_t = query.T
            QM[j, rows] = jnp.where(low, query, 0.0).astype(BF16)
            DOM[j, rows] = up.astype(BF16)
            DOT[j, c] = up.T.astype(BF16)
            QXT[j, c] = jnp.where(row128 < 64, query_t, QXT[j, c].astype(F32)).astype(BF16)
            if c == 0:
                QXT32[j] = jnp.where(row128 < 64, query_t, QXT32[j].astype(F32)).astype(BF16)

    def wide(ref, j, b):
        return jnp.concatenate([ref[j, 4 * b + i] for i in range(4)], axis=1)

    def forward(level, j, qxt, weights):
        sc = nn(KX[level, j], qxt)
        m = jnp.max(sc, axis=0, keepdims=True)
        w = jnp.exp(sc - m)
        weights[...] = w
        total = jnp.sum(w, axis=0, keepdims=True)
        o = nn(KVT[level, j, 64:128], w.astype(BF16))
        return m, total, o

    def backward(level, j, weights, factor, delta, dot_t, rows):
        p = weights[...] * factor
        dp = nn(natural(level, j), dot_t)
        ds = (p * (dp - delta)).astype(BF16)
        return nn(ds, QM[j, rows]) + nn(p.astype(BF16), DOM[j, rows]), nn(KVT[level, j, 0:64], ds)

    def out_copy(i, src, row, n, k):
        return pltpu.make_async_remote_copy(
            src_ref=src.at[head_peer(k)], dst_ref=out_ref.at[h, pl.ds(row, n)],
            send_sem=out_ss.at[i * 7 + k - 1], recv_sem=out_rs.at[i * 7 + k - 1],
            device_id={"head": head_peer(k)}, device_id_type=MESH)

    def out_local(i, src, row, n):
        return pltpu.make_async_copy(src.at[h], out_ref.at[h, pl.ds(row, n)], out_loc.at[i])

    def og_part(row, n):
        return og.at[:, pl.ds(row, n)]

    parts = []
    for j in range(2):
        parts += [(ROW_Q[j][0], 64), (ROW_Q[j][1], 64), (ROW_KV[j], 128), (ROW_T8[j], 16)]

    def start_out(i):
        row, n = parts[i]
        for k in range(1, NH):
            out_copy(i, og_part(row, n), row, n, k).start()
        out_local(i, og_part(row, n), row, n).start()

    def tz_copy(j, k):
        return pltpu.make_async_remote_copy(
            src_ref=og.at[head_peer(k), pl.ds(ROW_TZ[j], 16)], dst_ref=out_ref.at[h, pl.ds(ROW_TZ[j], 16)],
            send_sem=tz_ss.at[8 * j + k], recv_sem=tz_rs.at[8 * j + k],
            device_id={"seq": zpeer, "head": head_peer(k)}, device_id_type=MESH)

    def send_rows(i, top, bottom):
        row = parts[i][0]
        both = jnp.concatenate([top, bottom], axis=0).T.astype(BF16)
        og[:, row:row + 16] = both[0:128].reshape(8, 16, 128)
        og[:, row + 16:row + 64] = both[128:512].reshape(8, 48, 128)
        start_out(i)

    def g32_copy(j, k):
        return pltpu.make_async_remote_copy(
            src_ref=g32.at[j, k], dst_ref=r32.at[j, 16 - k],
            send_sem=l32_ss.at[29 + 15 * j + k], recv_sem=l32_rs.at[29 + 15 * j + k],
            device_id={"seq": plane_peer(k)}, device_id_type=MESH)

    def g8_copy(j, k):
        return pltpu.make_async_remote_copy(
            src_ref=g8.at[j, k], dst_ref=r8.at[j, 8 - k],
            send_sem=l8_ss.at[13 + 7 * j + k], recv_sem=l8_rs.at[13 + 7 * j + k],
            device_id={"seq": oct_peer(k)}, device_id_type=MESH)

    def g2_copy(j):
        return pltpu.make_async_remote_copy(
            src_ref=g2.at[j], dst_ref=r2.at[j], send_sem=l2_ss.at[2 + j], recv_sem=l2_rs.at[2 + j],
            device_id={"seq": pair}, device_id_type=MESH)

    put_row, put_col = iota((128, 32), 0), iota((128, 32), 1)
    put = (put_row == (put_col >> 2) * 16 + (put_col & 3)).astype(F32).astype(BF16)

    def send_keys(j):
        g2_copy(j).wait()
        for b in range(8):
            t2 = ACC[1, j, b * 64:b * 64 + 64] + r2[j, b].astype(F32)
            own = ACC[0, j, b * 128:b * 128 + 128]
            og[b, ROW_KV[j]:ROW_KV[j] + 64] = (own[0:64] + t2).astype(BF16)
            og[b, ROW_KV[j] + 64:ROW_KV[j] + 128] = own[64:128].astype(BF16)
        start_out(4 * j + 2)

    def spread(x):
        hi = x.astype(BF16)
        return nn(put, hi) + nn(put, (x - hi.astype(F32)).astype(BF16))

    def send_tiles(j):
        for k in range(1, 16):
            g32_copy(j, k).wait()
        mine, theirs = ACC[3, j, 0:32], ACC[3, j, 32:64]
        for m in range(1, 16):
            mine += r32[j, m, 0].astype(F32)
            theirs += r32[j, m, 1].astype(F32)
        og[:, ROW_TZ[j]:ROW_TZ[j] + 16] = spread(theirs).astype(BF16).reshape(8, 16, 128)
        for k in range(NH):
            tz_copy(j, k).start()
        for k in range(1, 8):
            g8_copy(j, k).wait()
        t8 = ACC[2, j, 0:128] + spread(mine)
        for m in range(1, 8):
            t8 += r8[j, m].astype(F32)
        og[:, ROW_T8[j]:ROW_T8[j] + 16] = t8.astype(BF16).reshape(8, 16, 128)
        start_out(4 * j + 3)

    def prepare_local(j):
        prepare(0, j, lambda c: inbuf[2 * j, c])

    def row_delta(j, part, o):
        return jnp.sum(wide(DOT, j, part)[64:128].astype(F32) * o, axis=0, keepdims=True)

    def attend_other(j):
        prepare_queries(j, 1)
        _, total, o = forward(0, j, wide(QXT, j, 1), W1)
        factor = 1.0 / total
        o = o * factor
        acc, dq = backward(0, j, W1, factor, row_delta(j, 1, o), wide(DOT, j, 1), slice(512, 1024))
        ACC[0, j] = acc if j == 0 else ACC[0, j] + acc
        send_rows(4 * j + 1, dq * 0.125, o)

    def attend_own(j, between):
        m1, l1, o1 = forward(0, j, wide(QXT, j, 0), W1)
        between()
        l2_copy(j).wait()
        prepare(1, j, lambda c: kv2[j, c // 4, pl.ds((c % 4) * 2, 2)].reshape(128, 128))
        m2, l2, o2 = forward(1, j, wide(QXT, j, 0), W2)
        for k in range(1, 8):
            l8_copy(j, k).wait()
        prepare(2, j, lambda c: kv8[j, c].reshape(128, 128))
        m3, l3, o3 = forward(2, j, QXT[j, 0], W8)
        for k in range(1, 16):
            l32_copy(j, k).wait()
        prepare(3, j, lambda c: kv32[j, pl.ds(2 * c, 2)].reshape(128, 128))
        m4, l4, o4 = forward(3, j, QXT32[j], W32)

        def on_first(x, f):
            return jnp.concatenate([f(x[:, 0:128]), x[:, 128:512]], axis=1)

        top = on_first(jnp.maximum(m1, m2), lambda x: jnp.maximum(x, jnp.maximum(m3, m4)))
        e1, e2 = jnp.exp(m1 - top), jnp.exp(m2 - top)
        e3, e4 = jnp.exp(m3 - top[:, 0:128]), jnp.exp(m4 - top[:, 0:128])
        factor = 1.0 / on_first(l1 * e1 + l2 * e2, lambda x: x + l3 * e3 + l4 * e4)
        o = on_first(o1 * e1 + o2 * e2, lambda x: x + o3 * e3 + o4 * e4) * factor
        delta = row_delta(j, 0, o)
        short = factor[:, 0:128], delta[:, 0:128]

        ACC[1, j], dq2 = backward(1, j, W2, e2 * factor, delta, wide(DOT, j, 0), slice(0, 512))
        g2[j] = ACC[1, j, 512:1024].reshape(8, 64, 128).astype(BF16)
        g2_copy(j).start()
        ACC[3, j], dq4 = backward(3, j, W32, e4 * short[0], short[1], DOT[j, 0], slice(0, 128))
        g32[j] = ACC[3, j].reshape(16, 2, 32, 128).astype(BF16)
        for k in range(1, 16):
            g32_copy(j, k).start()
        ACC[2, j], dq3 = backward(2, j, W8, e3 * short[0], short[1], DOT[j, 0], slice(0, 128))
        g8[j] = ACC[2, j].reshape(8, 128, 128).astype(BF16)
        for k in range(1, 8):
            g8_copy(j, k).start()
        acc, dq1 = backward(0, j, W1, e1 * factor, delta, wide(DOT, j, 0), slice(0, 512))
        ACC[0, j] = acc if j == 1 else ACC[0, j] + acc
        send_rows(4 * j, on_first(dq1 + dq2, lambda x: x + dq3 + dq4) * 0.125, o)

    wait_in(0)
    start_levels(0)
    prepare_local(0)
    wait_in(1)
    attend_other(0)
    wait_in(2)
    start_levels(1)
    prepare_local(1)
    wait_in(3)
    prepare_queries(0, 0)
    attend_own(0, lambda: None)
    wait_in(4)
    prepare_queries(1, 0)
    attend_own(1, lambda: send_keys(0))
    send_tiles(0)
    wait_in(5)
    attend_other(1)
    send_keys(1)
    send_tiles(1)

    for i in range(6):
        for k in range(1, NH):
            in_copy(i, k).wait_send()
    for j in range(2):
        for k in range(NH):
            zin_copy(j, k).wait_send()
            tz_copy(j, k).wait()
    for i, (row, n) in enumerate(parts):
        for k in range(1, NH):
            out_copy(i, og_part(row, n), row, n, k).wait()
        out_local(i, og_part(row, n), row, n).wait()


def restore_kernel(packed_ref, a_ref, q_ref, k_ref, v_ref):
    low = iota((128, 128), 1) < 64
    for g in range(NH):
        rho = iota((NB, NB), 1)
        mat = (iota((NB, NB), 0) == token_of(rho >> 6, rho & 63, g)).astype(F32).astype(BF16)
        cols = []
        for j in range(2):
            both = [packed_ref[g, row:row + 64] for row in ROW_Q[j]]
            cols.append(jnp.concatenate(both[::-1] if j else both, axis=0))
        for j in range(2):
            tile = sum(packed_ref[g, row:row + 16].astype(F32) for row in (ROW_KV[j], ROW_T8[j], ROW_TZ[j]))
            own = [tile.astype(BF16), packed_ref[g, ROW_KV[j] + 16:ROW_KV[j] + 64]]
            other = [packed_ref[g, ROW_KV[j] + 64:ROW_KV[j] + 128]]
            cols.append(jnp.concatenate(other + own if j else own + other, axis=0))
        res = nn(mat, jnp.concatenate(cols, axis=1))
        here = slice(g * 128, g * 128 + 128)
        for first, second, at in ((q_ref, a_ref, 0), (k_ref, v_ref, 256)):
            x, y = res[:, at:at + 128], res[:, at + 128:at + 256]
            first[:, here] = jnp.where(low, x, pltpu.roll(y, 64, 1)).astype(BF16)
            second[:, here] = jnp.where(low, pltpu.roll(x, 64, 1), y).astype(BF16)


def body(queries, keys, values, grad_out, doc_ids):
    vmem = pl.BlockSpec(memory_space=pltpu.VMEM)
    dma = pltpu.SemaphoreType.DMA
    packed = pl.pallas_call(
        attend_kernel,
        out_shape=jax.ShapeDtypeStruct((NH, ROWS, 128), BF16),
        in_specs=[pl.BlockSpec(memory_space=pl.ANY)] * 5,
        out_specs=pl.BlockSpec(memory_space=pl.ANY),
        scratch_shapes=[pltpu.VMEM(queries.shape, BF16)] * 4 + [
            pltpu.VMEM((256, 128), I32),
            pltpu.VMEM((4, NH, NB, 128), BF16),
            pltpu.VMEM((4, NH, NB, 128), BF16),
            pltpu.VMEM((2, 8, 16, 128), BF16),
            pltpu.VMEM((2, 2, 8, 64, 128), BF16),
            pltpu.VMEM((2, 8, 8, 16, 128), BF16),
            pltpu.VMEM((2, 16, 2, 32, 128), BF16),
            pltpu.VMEM((4, 2, 1024, 128), BF16),
            pltpu.VMEM((4, 2, 128, 1024), BF16),
            pltpu.VMEM((512, 128), BF16),
            pltpu.VMEM((2, 8, 128, 128), BF16),
            pltpu.VMEM((2, 128, 128), BF16),
            pltpu.VMEM((2, 1024, 128), BF16),
            pltpu.VMEM((2, 1024, 128), BF16),
            pltpu.VMEM((2, 8, 128, 128), BF16),
            pltpu.VMEM((1024, 512), F32),
            pltpu.VMEM((1024, 512), F32),
            pltpu.VMEM((1024, 128), F32),
            pltpu.VMEM((1024, 128), F32),
            pltpu.VMEM((4, 2, 1024, 128), F32),
            pltpu.VMEM((2, 8, 64, 128), BF16),
            pltpu.VMEM((2, 8, 64, 128), BF16),
            pltpu.VMEM((2, 8, 128, 128), BF16),
            pltpu.VMEM((2, 8, 128, 128), BF16),
            pltpu.VMEM((2, 16, 2, 32, 128), BF16),
            pltpu.VMEM((2, 16, 2, 32, 128), BF16),
            pltpu.VMEM((NH, ROWS, 128), BF16),
            dma((5,)), dma((42,)), dma((42,)), dma((16,)), dma((16,)), dma((6,)),
            dma((4,)), dma((4,)), dma((28,)), dma((28,)), dma((60,)), dma((60,)),
            dma((56,)), dma((56,)), dma((16,)), dma((16,)), dma((8,)),
        ],
        compiler_params=pltpu.CompilerParams(
            collective_id=0, has_side_effects=True, vmem_limit_bytes=56 * 1024 * 1024),
        name="attend",
    )(queries, keys, values, grad_out, doc_ids.reshape(256, 128))
    shape = jax.ShapeDtypeStruct(queries.shape, BF16)
    return pl.pallas_call(
        restore_kernel,
        out_shape=(shape, shape, shape, shape),
        in_specs=[vmem],
        out_specs=(vmem, vmem, vmem, vmem),
        compiler_params=pltpu.CompilerParams(vmem_limit_bytes=32 * 1024 * 1024),
        name="restore",
    )(packed)


def solution(mesh):
    spec = P(("seq", "head"), None)
    return jax.shard_map(
        body, mesh=mesh, in_specs=(spec, spec, spec, spec, P()), out_specs=(spec, spec, spec, spec), check_vma=False)
```

```python
import jax
import jax.numpy as jnp
from jax import lax
from jax.experimental import pallas as pl
from jax.experimental.pallas import tpu as pltpu
from jax.sharding import PartitionSpec as P

F32 = jnp.float32
BF16 = jnp.bfloat16
I32 = jnp.int32
BIG = 1e30
NH = 8
NB = 128
MESH = pl.DeviceIdType.MESH
ROW_Q, ROW_KV, ROW_TZ, ROWS = ((0, 64), (128, 192)), (256, 384), 512, 528


def iota(shape, dim):
    return lax.broadcasted_iota(I32, shape, dim)


def token_of(parity, w, h):
    t, u, a = (w >> 4) & 3, (w >> 2) & 3, w & 3
    return a * 32 + parity + 2 * ((h + t) & 3) + 8 * ((h // 4 + u) & 3)


def nn(a, b):
    return lax.dot_general(a, b, (((1,), (0,)), ((), ())), preferred_element_type=F32)


def attend_kernel(
    q_hbm, k_hbm, v_hbm, do_hbm, docs_hbm, out_ref,
    q_ref, k_ref, v_ref, do_ref, docs_ref,
    send, zsend, inbuf, zin, kv2, kv8, kv32, KX, KVT, QG, QXT, QXT32, QM, DOM, DOT,
    WB, W1, W2, W8, W32, ACC, g2, r2, g8, r8, g32, r32, og,
    load_s, in_ss, in_rs, zin_ss, zin_rs, loc_s, l2_ss, l2_rs, l8_ss, l8_rs, l32_ss, l32_rs,
    out_ss, out_rs, tz_ss, tz_rs, out_loc,
):
    h = lax.axis_index("head")
    s = lax.axis_index("seq")
    pair = s + 1 - 2 * (s % 2)
    base8 = (s // 8) * 8
    base16 = (s // 16) * 16
    zpeer = (s + 16) % 32

    def plane_peer(k):
        return base16 + (s - base16 + k) % 16

    def oct_peer(k):
        return base8 + (s - base8 + k) % 8

    def head_peer(k):
        return (h + k) % NH

    pairs = ((k_hbm, k_ref), (v_hbm, v_ref), (q_hbm, q_ref), (do_hbm, do_ref), (docs_hbm, docs_ref))
    loads = [pltpu.make_async_copy(a, b, load_s.at[i]) for i, (a, b) in enumerate(pairs)]
    for load in loads:
        load.start()

    barrier = pltpu.get_barrier_semaphore()
    for k in range(1, NH):
        pl.semaphore_signal(barrier, inc=1, device_id={"head": head_peer(k)}, device_id_type=MESH)
    for k in range(1, 16):
        pl.semaphore_signal(barrier, inc=1, device_id={"seq": plane_peer(k)}, device_id_type=MESH)
    for k in range(NH):
        pl.semaphore_signal(barrier, inc=1, device_id={"seq": zpeer, "head": head_peer(k)}, device_id_type=MESH)

    lane128 = iota((128, 128), 1)
    row128 = iota((128, 128), 0)
    low = lane128 < 64

    def permute_two(first, a_ref, b_ref):
        for g in range(NH):
            mat = (lane128 == token_of(row128 >> 6, row128 & 63, g)).astype(F32).astype(BF16)
            cols = slice(g * 128, g * 128 + 128)
            res = nn(mat, jnp.concatenate([a_ref[:, cols], b_ref[:, cols]], axis=1))
            a, b = res[:, 0:128], res[:, 128:256]
            one = jnp.where(low, a, pltpu.roll(b, 64, 1))
            other = jnp.where(low, pltpu.roll(a, 64, 1), b)
            send[first, g] = one.astype(BF16)
            send[first + 2, g, 0:64] = other[64:128].astype(BF16)
            send[first + 2, g, 64:128] = other[0:64].astype(BF16)
            if first == 0:
                zsend[g] = jnp.where(row128[0:16] < 4, one[0:16], pltpu.roll(other[64:80], 4, 0)).astype(BF16)

    messages = ((0, 0, 128), (1, 0, 64), (1, 64, 64), (2, 0, 128), (3, 0, 64), (3, 64, 64))

    def in_copy(i, k):
        t, row, n = messages[i]
        return pltpu.make_async_remote_copy(
            src_ref=send.at[t, head_peer(k), pl.ds(row, n)], dst_ref=inbuf.at[t, h, pl.ds(row, n)],
            send_sem=in_ss.at[i * 7 + k - 1], recv_sem=in_rs.at[i * 7 + k - 1],
            device_id={"head": head_peer(k)}, device_id_type=MESH)

    def in_local(i):
        t, row, n = messages[i]
        return pltpu.make_async_copy(
            send.at[t, h, pl.ds(row, n)], inbuf.at[t, h, pl.ds(row, n)], loc_s.at[i])

    def start_in(i):
        for k in range(1, NH):
            in_copy(i, k).start()
        in_local(i).start()

    def wait_in(i):
        for k in range(1, NH):
            in_copy(i, k).wait_recv()
        in_local(i).wait()

    def zin_copy(k):
        return pltpu.make_async_remote_copy(
            src_ref=zsend.at[head_peer(k)], dst_ref=zin.at[h],
            send_sem=zin_ss.at[k], recv_sem=zin_rs.at[k],
            device_id={"seq": zpeer, "head": head_peer(k)}, device_id_type=MESH)

    loads[0].wait()
    loads[1].wait()
    permute_two(0, k_ref, v_ref)
    pl.semaphore_wait(barrier, 30)
    for k in range(NH):
        zin_copy(k).start()
    start_in(0)
    loads[2].wait()
    loads[3].wait()
    permute_two(1, q_ref, do_ref)
    for i in range(1, 6):
        start_in(i)
    loads[4].wait()

    docs = docs_ref[...]

    def count(limit):
        c = jnp.sum((docs < limit).astype(F32), axis=0, keepdims=True)
        return jnp.sum(c, axis=1, keepdims=True).astype(I32)

    bound1, bound2 = count(1), count(2)

    def doc_of(pos):
        return (pos >= bound1).astype(I32) + (pos >= bound2).astype(I32)

    def key_place(level, c):
        r = row128 + c * 128
        if level == 0:
            return s, r >> 7, r & 127
        if level == 1:
            return jnp.where((r >> 9) == 0, s, pair), (r >> 6) & 7, r & 63
        if level == 2:
            return base8 + ((s + (r >> 7)) & 7), (r >> 4) & 7, r & 15
        plane = jnp.where(((r >> 5) & 1) == 0, base16, 16 - base16)
        return plane + ((s + (r >> 6)) & 15), (r >> 2) & 7, r & 3

    def fill_features(c, carry):
        for level in range(4):
            seqs, src, w = key_place(level, c)
            start = seqs * 1024 + src * 128
            for j in range(2):
                parity = j ^ (w >> 6)
                doc = doc_of(start + token_of(parity, w & 63, h))
                hot = (lane128 - 64 == doc) | (lane128 == 67)
                KX[level, j, pl.ds(c * 128, 128)] = jnp.where(hot, 1.0, 0.0).astype(BF16)
        return carry

    lax.fori_loop(0, 8, fill_features, 0)

    feat_row = row128 - 64
    for c in range(8):
        if c % 4 == 0:
            src, w = lane128 >> 4, lane128 & 15
        else:
            i = lane128 + (c % 4 - 1) * 128
            src = (i * 1366) >> 16
            w = 16 + i - src * 48
        w = w + 64 * (c // 4)
        for j in range(2):
            parity = j ^ (w >> 6)
            doc = doc_of(s * 1024 + src * 128 + token_of(parity, w & 63, h))
            hide = (feat_row >= 0) & (feat_row < 3) & (feat_row != doc)
            QXT[j, c] = jnp.where(hide, -BIG, 0.0).astype(BF16)
            if c == 0:
                hide = hide | ((feat_row == 3) & (w >= 4))
                QXT32[j] = jnp.where(hide, -BIG, 0.0).astype(BF16)

    def l2_copy(j):
        return pltpu.make_async_remote_copy(
            src_ref=inbuf.at[2 * j, :, pl.ds(0, 64), :], dst_ref=kv2.at[j, 1],
            send_sem=l2_ss.at[j], recv_sem=l2_rs.at[j], device_id={"seq": pair}, device_id_type=MESH)

    def l8_copy(j, k):
        return pltpu.make_async_remote_copy(
            src_ref=inbuf.at[2 * j, :, pl.ds(0, 16), :], dst_ref=kv8.at[j, 8 - k],
            send_sem=l8_ss.at[7 * j + k - 1], recv_sem=l8_rs.at[7 * j + k - 1],
            device_id={"seq": oct_peer(k)}, device_id_type=MESH)

    def l32_copy(j, k):
        return pltpu.make_async_remote_copy(
            src_ref=kv32.at[j, 0], dst_ref=kv32.at[j, 16 - k],
            send_sem=l32_ss.at[15 * j + k - 1], recv_sem=l32_rs.at[15 * j + k - 1],
            device_id={"seq": plane_peer(k)}, device_id_type=MESH)

    def pick(j):
        row, col = iota((32, 128), 0), iota((32, 128), 1)
        return (col == (row >> 2) * 16 + (row & 3) + 4 * j).astype(F32).astype(BF16)

    def start_levels(j):
        l2_copy(j).start()
        for k in range(1, 8):
            l8_copy(j, k).start()
        if j == 0:
            for k in range(NH):
                zin_copy(k).wait_recv()
        kv32[j, 0, 0] = nn(pick(0), inbuf[2 * j, :, 0:16].reshape(128, 128)).astype(BF16)
        kv32[j, 0, 1] = nn(pick(j), zin[...].reshape(128, 128)).astype(BF16)
        for k in range(1, 16):
            l32_copy(j, k).start()
        kv2[j, 0] = inbuf[2 * j, :, 0:64]
        kv8[j, 0] = inbuf[2 * j, :, 0:16]

    def prepare(level, j, load):
        for c in range(8):
            rows = slice(c * 128, c * 128 + 128)
            kv = load(c).astype(F32)
            KX[level, j, rows] = jnp.where(low, kv, KX[level, j, rows].astype(F32)).astype(BF16)
            KVT[level, j, :, rows] = kv.T.astype(BF16)

    def natural(level, j):
        ref = (inbuf.at[2 * j], kv2.at[j], kv8.at[j], kv32.at[j])[level]
        return ref[...].reshape(1024, 128)

    def prepare_queries(j, part):
        x = inbuf.at[2 * j + 1, :, pl.ds(64 * part, 64)]
        QG[0:128] = x[:, 0:16].reshape(128, 128)
        QG[128:512] = x[:, 16:64].reshape(384, 128)
        for i in range(4):
            c = 4 * part + i
            rows = slice(c * 128, c * 128 + 128)
            qd = QG[i * 128:i * 128 + 128].astype(F32)
            query, up = qd * 0.125, jnp.where(low, 0.0, qd)
            query_t = query.T
            QM[j, rows] = jnp.where(low, query, 0.0).astype(BF16)
            DOM[j, rows] = up.astype(BF16)
            DOT[j, c] = up.T.astype(BF16)
            QXT[j, c] = jnp.where(row128 < 64, query_t, QXT[j, c].astype(F32)).astype(BF16)
            if c == 0:
                QXT32[j] = jnp.where(row128 < 64, query_t, QXT32[j].astype(F32)).astype(BF16)

    def wide(ref, j, b):
        return jnp.concatenate([ref[j, 4 * b + i] for i in range(4)], axis=1)

    def forward(level, j, qxt, weights):
        sc = nn(KX[level, j], qxt)
        m = jnp.max(sc, axis=0, keepdims=True)
        w = jnp.exp(sc - m)
        weights[...] = w
        total = jnp.sum(w, axis=0, keepdims=True)
        o = nn(KVT[level, j, 64:128], w.astype(BF16))
        return m, total, o

    def backward(level, j, weights, factor, delta, dot_t, rows):
        p = weights[...] * factor
        dp = nn(natural(level, j), dot_t)
        ds = (p * (dp - delta)).astype(BF16)
        return nn(ds, QM[j, rows]) + nn(p.astype(BF16), DOM[j, rows]), nn(KVT[level, j, 0:64], ds)

    def out_copy(i, src, row, n, k):
        return pltpu.make_async_remote_copy(
            src_ref=src.at[head_peer(k)], dst_ref=out_ref.at[h, pl.ds(row, n)],
            send_sem=out_ss.at[i * 7 + k - 1], recv_sem=out_rs.at[i * 7 + k - 1],
            device_id={"head": head_peer(k)}, device_id_type=MESH)

    def out_local(i, src, row, n):
        return pltpu.make_async_copy(src.at[h], out_ref.at[h, pl.ds(row, n)], out_loc.at[i])

    def og_part(row, n):
        return og.at[:, pl.ds(row, n)]

    parts = []
    for j in range(2):
        parts += [(ROW_Q[j][0], 64), (ROW_Q[j][1], 64), (ROW_KV[j] + 16, 112), (ROW_KV[j], 16)]

    def start_out(i):
        row, n = parts[i]
        for k in range(1, NH):
            out_copy(i, og_part(row, n), row, n, k).start()
        out_local(i, og_part(row, n), row, n).start()

    def tz_copy(k):
        return pltpu.make_async_remote_copy(
            src_ref=og.at[head_peer(k), pl.ds(ROW_TZ, 16)], dst_ref=out_ref.at[h, pl.ds(ROW_TZ, 16)],
            send_sem=tz_ss.at[k], recv_sem=tz_rs.at[k],
            device_id={"seq": zpeer, "head": head_peer(k)}, device_id_type=MESH)

    def send_rows(i, top, bottom):
        row = parts[i][0]
        both = jnp.concatenate([top, bottom], axis=0).T.astype(BF16)
        og[:, row:row + 16] = both[0:128].reshape(8, 16, 128)
        og[:, row + 16:row + 64] = both[128:512].reshape(8, 48, 128)
        start_out(i)

    def g32_copy(j, k):
        return pltpu.make_async_remote_copy(
            src_ref=g32.at[j, k], dst_ref=r32.at[j, 16 - k],
            send_sem=l32_ss.at[29 + 15 * j + k], recv_sem=l32_rs.at[29 + 15 * j + k],
            device_id={"seq": plane_peer(k)}, device_id_type=MESH)

    def g8_copy(j, k):
        return pltpu.make_async_remote_copy(
            src_ref=g8.at[j, k], dst_ref=r8.at[j, 8 - k],
            send_sem=l8_ss.at[13 + 7 * j + k], recv_sem=l8_rs.at[13 + 7 * j + k],
            device_id={"seq": oct_peer(k)}, device_id_type=MESH)

    def g2_copy(j):
        return pltpu.make_async_remote_copy(
            src_ref=g2.at[j], dst_ref=r2.at[j], send_sem=l2_ss.at[2 + j], recv_sem=l2_rs.at[2 + j],
            device_id={"seq": pair}, device_id_type=MESH)

    def put(j):
        row, col = iota((128, 32), 0), iota((128, 32), 1)
        return (row == (col >> 2) * 16 + (col & 3) + 4 * j).astype(F32).astype(BF16)

    def spread(j, x):
        hi = x.astype(BF16)
        return nn(put(j), hi) + nn(put(j), (x - hi.astype(F32)).astype(BF16))

    def send_keys(j):
        g2_copy(j).wait()
        for b in range(8):
            t2 = ACC[1, j, b * 64 + 16:b * 64 + 64] + r2[j, b, 16:64].astype(F32)
            own = ACC[0, j, b * 128 + 16:b * 128 + 128]
            og[b, ROW_KV[j] + 16:ROW_KV[j] + 64] = (own[0:48] + t2).astype(BF16)
            og[b, ROW_KV[j] + 64:ROW_KV[j] + 128] = own[48:112].astype(BF16)
        start_out(4 * j + 2)

    def sum_plane(j):
        for k in range(1, 16):
            g32_copy(j, k).wait()
        total = ACC[3, j, 0:64]
        for m in range(1, 16):
            total += r32[j, m].reshape(64, 128).astype(F32)
        ACC[3, j, 0:64] = total

    def send_tiles(j):
        for k in range(1, 8):
            g8_copy(j, k).wait()
        t8 = ACC[2, j, 0:128] + spread(0, ACC[3, j, 0:32])
        for m in range(1, 8):
            t8 += r8[j, m].astype(F32)
        for b in range(8):
            t2 = ACC[1, j, b * 64:b * 64 + 16] + r2[j, b, 0:16].astype(F32)
            own = ACC[0, j, b * 128:b * 128 + 16]
            og[b, ROW_KV[j]:ROW_KV[j] + 16] = (own + t2 + t8[b * 16:b * 16 + 16]).astype(BF16)
        start_out(4 * j + 3)

    def send_plane():
        both = spread(0, ACC[3, 0, 32:64]) + spread(1, ACC[3, 1, 32:64])
        og[:, ROW_TZ:ROW_TZ + 16] = both.astype(BF16).reshape(8, 16, 128)
        for k in range(NH):
            tz_copy(k).start()

    def prepare_local(j):
        prepare(0, j, lambda c: inbuf[2 * j, c])

    def row_delta(j, part, o):
        return jnp.sum(wide(DOT, j, part)[64:128].astype(F32) * o, axis=0, keepdims=True)

    def attend_other(j):
        prepare_queries(j, 1)
        _, total, o = forward(0, j, wide(QXT, j, 1), WB)
        factor = 1.0 / total
        o = o * factor
        acc, dq = backward(0, j, WB, factor, row_delta(j, 1, o), wide(DOT, j, 1), slice(512, 1024))
        ACC[0, j] = acc
        send_rows(4 * j + 1, dq * 0.125, o)

    def attend_own(j, before, after):
        m1, l1, o1 = forward(0, j, wide(QXT, j, 0), W1)
        before()
        l2_copy(j).wait()
        prepare(1, j, lambda c: kv2[j, c // 4, c % 4 * 2:c % 4 * 2 + 2].reshape(128, 128))
        m2, l2, o2 = forward(1, j, wide(QXT, j, 0), W2)
        for k in range(1, 8):
            l8_copy(j, k).wait()
        prepare(2, j, lambda c: kv8[j, c].reshape(128, 128))
        m3, l3, o3 = forward(2, j, QXT[j, 0], W8)
        for k in range(1, 16):
            l32_copy(j, k).wait()
        prepare(3, j, lambda c: kv32[j, 2 * c:2 * c + 2].reshape(128, 128))
        m4, l4, o4 = forward(3, j, QXT32[j], W32)

        def on_first(x, f):
            return jnp.concatenate([f(x[:, 0:128]), x[:, 128:512]], axis=1)

        top = on_first(jnp.maximum(m1, m2), lambda x: jnp.maximum(x, jnp.maximum(m3, m4)))
        e1, e2 = jnp.exp(m1 - top), jnp.exp(m2 - top)
        e3, e4 = jnp.exp(m3 - top[:, 0:128]), jnp.exp(m4 - top[:, 0:128])
        factor = 1.0 / on_first(l1 * e1 + l2 * e2, lambda x: x + l3 * e3 + l4 * e4)
        o = on_first(o1 * e1 + o2 * e2, lambda x: x + o3 * e3 + o4 * e4) * factor
        delta = row_delta(j, 0, o)
        short = factor[:, 0:128], delta[:, 0:128]

        ACC[1, j], dq2 = backward(1, j, W2, e2 * factor, delta, wide(DOT, j, 0), slice(0, 512))
        g2[j] = ACC[1, j, 512:1024].reshape(8, 64, 128).astype(BF16)
        g2_copy(j).start()
        after()
        ACC[3, j], dq4 = backward(3, j, W32, e4 * short[0], short[1], DOT[j, 0], slice(0, 128))
        g32[j] = ACC[3, j].reshape(16, 2, 32, 128).astype(BF16)
        for k in range(1, 16):
            g32_copy(j, k).start()
        ACC[2, j], dq3 = backward(2, j, W8, e3 * short[0], short[1], DOT[j, 0], slice(0, 128))
        g8[j] = ACC[2, j].reshape(8, 128, 128).astype(BF16)
        for k in range(1, 8):
            g8_copy(j, k).start()
        acc, dq1 = backward(0, j, W1, e1 * factor, delta, wide(DOT, j, 0), slice(0, 512))
        ACC[0, j] += acc
        send_rows(4 * j, on_first(dq1 + dq2, lambda x: x + dq3 + dq4) * 0.125, o)

    def other_first():
        wait_in(2)
        attend_other(0)

    def other_second():
        send_keys(0)
        wait_in(5)
        attend_other(1)

    def next_levels():
        wait_in(3)
        start_levels(1)

    wait_in(0)
    start_levels(0)
    prepare_local(0)
    wait_in(1)
    prepare_queries(0, 0)
    attend_own(0, other_first, next_levels)
    prepare_local(1)
    wait_in(4)
    prepare_queries(1, 0)
    attend_own(1, other_second, lambda: None)
    sum_plane(0)
    send_tiles(0)
    send_keys(1)
    sum_plane(1)
    send_plane()
    send_tiles(1)

    for i in range(6):
        for k in range(1, NH):
            in_copy(i, k).wait_send()
    for k in range(NH):
        zin_copy(k).wait_send()
        tz_copy(k).wait()
    for i, (row, n) in enumerate(parts):
        for k in range(1, NH):
            out_copy(i, og_part(row, n), row, n, k).wait()
        out_local(i, og_part(row, n), row, n).wait()


def restore_kernel(packed_ref, a_ref, q_ref, k_ref, v_ref):
    low = iota((128, 128), 1) < 64
    first4 = iota((16, 128), 0) < 4
    for g in range(NH):
        rho = iota((NB, NB), 1)
        mat = (iota((NB, NB), 0) == token_of(rho >> 6, rho & 63, g)).astype(F32).astype(BF16)
        cols = []
        for j in range(2):
            both = [packed_ref[g, row:row + 64] for row in ROW_Q[j]]
            cols.append(jnp.concatenate(both[::-1] if j else both, axis=0))
        for j in range(2):
            plane = packed_ref[g, ROW_TZ:ROW_TZ + 16].astype(F32)
            plane = jnp.where(first4, pltpu.roll(plane, 12, 0) if j else plane, 0.0)
            tile = packed_ref[g, ROW_KV[j]:ROW_KV[j] + 16].astype(F32) + plane
            own = [tile.astype(BF16), packed_ref[g, ROW_KV[j] + 16:ROW_KV[j] + 64]]
            other = [packed_ref[g, ROW_KV[j] + 64:ROW_KV[j] + 128]]
            cols.append(jnp.concatenate(other + own if j else own + other, axis=0))
        res = nn(mat, jnp.concatenate(cols, axis=1))
        here = slice(g * 128, g * 128 + 128)
        for first, second, at in ((q_ref, a_ref, 0), (k_ref, v_ref, 256)):
            x, y = res[:, at:at + 128], res[:, at + 128:at + 256]
            first[:, here] = jnp.where(low, x, pltpu.roll(y, 64, 1)).astype(BF16)
            second[:, here] = jnp.where(low, pltpu.roll(x, 64, 1), y).astype(BF16)


def body(queries, keys, values, grad_out, doc_ids):
    vmem = pl.BlockSpec(memory_space=pltpu.VMEM)
    dma = pltpu.SemaphoreType.DMA
    packed = pl.pallas_call(
        attend_kernel,
        out_shape=jax.ShapeDtypeStruct((NH, ROWS, 128), BF16),
        in_specs=[pl.BlockSpec(memory_space=pl.ANY)] * 5,
        out_specs=pl.BlockSpec(memory_space=pl.ANY),
        scratch_shapes=[pltpu.VMEM(queries.shape, BF16)] * 4 + [
            pltpu.VMEM((256, 128), I32),
            pltpu.VMEM((4, NH, NB, 128), BF16),
            pltpu.VMEM((NH, 16, 128), BF16),
            pltpu.VMEM((4, NH, NB, 128), BF16),
            pltpu.VMEM((NH, 16, 128), BF16),
            pltpu.VMEM((2, 2, 8, 64, 128), BF16),
            pltpu.VMEM((2, 8, 8, 16, 128), BF16),
            pltpu.VMEM((2, 16, 2, 32, 128), BF16),
            pltpu.VMEM((4, 2, 1024, 128), BF16),
            pltpu.VMEM((4, 2, 128, 1024), BF16),
            pltpu.VMEM((512, 128), BF16),
            pltpu.VMEM((2, 8, 128, 128), BF16),
            pltpu.VMEM((2, 128, 128), BF16),
            pltpu.VMEM((2, 1024, 128), BF16),
            pltpu.VMEM((2, 1024, 128), BF16),
            pltpu.VMEM((2, 8, 128, 128), BF16),
            pltpu.VMEM((1024, 512), F32),
            pltpu.VMEM((1024, 512), F32),
            pltpu.VMEM((1024, 512), F32),
            pltpu.VMEM((1024, 128), F32),
            pltpu.VMEM((1024, 128), F32),
            pltpu.VMEM((4, 2, 1024, 128), F32),
            pltpu.VMEM((2, 8, 64, 128), BF16),
            pltpu.VMEM((2, 8, 64, 128), BF16),
            pltpu.VMEM((2, 8, 128, 128), BF16),
            pltpu.VMEM((2, 8, 128, 128), BF16),
            pltpu.VMEM((2, 16, 2, 32, 128), BF16),
            pltpu.VMEM((2, 16, 2, 32, 128), BF16),
            pltpu.VMEM((NH, ROWS, 128), BF16),
            dma((5,)), dma((42,)), dma((42,)), dma((8,)), dma((8,)), dma((6,)),
            dma((4,)), dma((4,)), dma((28,)), dma((28,)), dma((60,)), dma((60,)),
            dma((56,)), dma((56,)), dma((8,)), dma((8,)), dma((8,)),
        ],
        compiler_params=pltpu.CompilerParams(
            collective_id=0, has_side_effects=True, vmem_limit_bytes=56 * 1024 * 1024),
        name="attend",
    )(queries, keys, values, grad_out, doc_ids.reshape(256, 128))
    shape = jax.ShapeDtypeStruct(queries.shape, BF16)
    return pl.pallas_call(
        restore_kernel,
        out_shape=(shape, shape, shape, shape),
        in_specs=[vmem],
        out_specs=(vmem, vmem, vmem, vmem),
        compiler_params=pltpu.CompilerParams(vmem_limit_bytes=32 * 1024 * 1024),
        name="restore",
    )(packed)


def solution(mesh):
    spec = P(("seq", "head"), None)
    return jax.shard_map(
        body, mesh=mesh, in_specs=(spec, spec, spec, spec, P()), out_specs=(spec, spec, spec, spec), check_vma=False)
```

```python
import jax
import jax.numpy as jnp
from jax import lax
from jax.experimental import pallas as pl
from jax.experimental.pallas import tpu as pltpu
from jax.sharding import PartitionSpec as P

F32 = jnp.float32
BF16 = jnp.bfloat16
I32 = jnp.int32
BIG = 1e30
NH = 8
NB = 128
MESH = pl.DeviceIdType.MESH
ROW_Q, ROW_KV, ROW_TZ, ROWS = ((0, 64), (128, 192)), (256, 384), 512, 528


def iota(shape, dim):
    return lax.broadcasted_iota(I32, shape, dim)


def token_of(parity, w, h):
    t, u, a = (w >> 4) & 3, (w >> 2) & 3, w & 3
    return a * 32 + parity + 2 * ((h + t) & 3) + 8 * ((h // 4 + u) & 3)


def nn(a, b):
    return lax.dot_general(a, b, (((1,), (0,)), ((), ())), preferred_element_type=F32)


def attend_kernel(
    q_hbm, k_hbm, v_hbm, do_hbm, docs_hbm, out_ref,
    q_ref, k_ref, v_ref, do_ref, docs_ref,
    send, zsend, inbuf, zin, kv2, kv8, kv32, KX, KVT, QG, QXT, QXT32, QM, DOM, DOT,
    WB, W1, W2, W8, W32, ACC, g2, r2, g8, r8, g32, r32, og,
    load_s, in_ss, in_rs, zin_ss, zin_rs, loc_s, l2_ss, l2_rs, l8_ss, l8_rs, l32_ss, l32_rs,
    out_ss, out_rs, tz_ss, tz_rs, out_loc,
):
    h = lax.axis_index("head")
    s = lax.axis_index("seq")
    pair = s + 1 - 2 * (s % 2)
    base8 = (s // 8) * 8
    base16 = (s // 16) * 16
    zpeer = (s + 16) % 32

    def plane_peer(k):
        return base16 + (s - base16 + k) % 16

    def oct_peer(k):
        return base8 + (s - base8 + k) % 8

    def head_peer(k):
        return (h + k) % NH

    pairs = ((k_hbm, k_ref), (v_hbm, v_ref), (q_hbm, q_ref), (do_hbm, do_ref), (docs_hbm, docs_ref))
    loads = [pltpu.make_async_copy(a, b, load_s.at[i]) for i, (a, b) in enumerate(pairs)]
    for load in loads:
        load.start()

    barrier = pltpu.get_barrier_semaphore()
    for k in range(1, NH):
        pl.semaphore_signal(barrier, inc=1, device_id={"head": head_peer(k)}, device_id_type=MESH)
    for k in range(1, 16):
        pl.semaphore_signal(barrier, inc=1, device_id={"seq": plane_peer(k)}, device_id_type=MESH)
    for k in range(NH):
        pl.semaphore_signal(barrier, inc=1, device_id={"seq": zpeer, "head": head_peer(k)}, device_id_type=MESH)

    lane128 = iota((128, 128), 1)
    row128 = iota((128, 128), 0)
    low = lane128 < 64

    def permute_two(first, a_ref, b_ref):
        for g in range(NH):
            mat = (lane128 == token_of(row128 >> 6, row128 & 63, g)).astype(F32).astype(BF16)
            cols = slice(g * 128, g * 128 + 128)
            res = nn(mat, jnp.concatenate([a_ref[:, cols], b_ref[:, cols]], axis=1))
            a, b = res[:, 0:128], res[:, 128:256]
            one = jnp.where(low, a, pltpu.roll(b, 64, 1))
            other = jnp.where(low, pltpu.roll(a, 64, 1), b)
            send[first, g] = one.astype(BF16)
            send[first + 2, g, 0:64] = other[64:128].astype(BF16)
            send[first + 2, g, 64:128] = other[0:64].astype(BF16)
            if first == 0:
                zsend[g] = jnp.where(row128[0:16] < 4, one[0:16], pltpu.roll(other[64:80], 4, 0)).astype(BF16)

    messages = tuple((t, row, 64) for t, row in (
        (0, 0), (2, 0), (0, 64), (1, 64), (1, 0), (2, 64), (3, 0), (3, 64)))

    def in_copy(i, k):
        t, row, n = messages[i]
        return pltpu.make_async_remote_copy(
            src_ref=send.at[t, head_peer(k), pl.ds(row, n)], dst_ref=inbuf.at[t, h, pl.ds(row, n)],
            send_sem=in_ss.at[i * 7 + k - 1], recv_sem=in_rs.at[i * 7 + k - 1],
            device_id={"head": head_peer(k)}, device_id_type=MESH)

    def in_local(i):
        t, row, n = messages[i]
        return pltpu.make_async_copy(
            send.at[t, h, pl.ds(row, n)], inbuf.at[t, h, pl.ds(row, n)], loc_s.at[i])

    def start_in(i):
        for k in range(1, NH):
            in_copy(i, k).start()
        in_local(i).start()

    def wait_in(i):
        for k in range(1, NH):
            in_copy(i, k).wait_recv()
        in_local(i).wait()

    def zin_copy(k):
        return pltpu.make_async_remote_copy(
            src_ref=zsend.at[head_peer(k)], dst_ref=zin.at[h],
            send_sem=zin_ss.at[k], recv_sem=zin_rs.at[k],
            device_id={"seq": zpeer, "head": head_peer(k)}, device_id_type=MESH)

    loads[0].wait()
    loads[1].wait()
    permute_two(0, k_ref, v_ref)
    pl.semaphore_wait(barrier, 30)
    for k in range(NH):
        zin_copy(k).start()
    for i in range(3):
        start_in(i)
    loads[2].wait()
    loads[3].wait()
    permute_two(1, q_ref, do_ref)
    for i in range(3, 8):
        start_in(i)
    loads[4].wait()

    docs = docs_ref[...]

    def count(limit):
        c = jnp.sum((docs < limit).astype(F32), axis=0, keepdims=True)
        return jnp.sum(c, axis=1, keepdims=True).astype(I32)

    bound1, bound2 = count(1), count(2)

    def doc_of(pos):
        return (pos >= bound1).astype(I32) + (pos >= bound2).astype(I32)

    def key_place(level, c):
        r = row128 + c * 128
        if level == 0:
            return s, r >> 7, r & 127
        if level == 1:
            return jnp.where((r >> 9) == 0, s, pair), (r >> 6) & 7, r & 63
        if level == 2:
            return base8 + ((s + (r >> 7)) & 7), (r >> 4) & 7, r & 15
        plane = jnp.where(((r >> 5) & 1) == 0, base16, 16 - base16)
        return plane + ((s + (r >> 6)) & 15), (r >> 2) & 7, r & 3

    def fill_features(c, carry):
        for level in range(4):
            seqs, src, w = key_place(level, c)
            start = seqs * 1024 + src * 128
            for j in range(2):
                parity = j ^ (w >> 6)
                doc = doc_of(start + token_of(parity, w & 63, h))
                hot = (lane128 - 64 == doc) | (lane128 == 67)
                KX[level, j, pl.ds(c * 128, 128)] = jnp.where(hot, 1.0, 0.0).astype(BF16)
        return carry

    lax.fori_loop(0, 8, fill_features, 0)

    feat_row = row128 - 64
    for c in range(8):
        if c % 4 == 0:
            src, w = lane128 >> 4, lane128 & 15
        else:
            i = lane128 + (c % 4 - 1) * 128
            src = (i * 1366) >> 16
            w = 16 + i - src * 48
        w = w + 64 * (c // 4)
        for j in range(2):
            parity = j ^ (w >> 6)
            doc = doc_of(s * 1024 + src * 128 + token_of(parity, w & 63, h))
            hide = (feat_row >= 0) & (feat_row < 3) & (feat_row != doc)
            QXT[j, c] = jnp.where(hide, -BIG, 0.0).astype(BF16)
            if c == 0:
                hide = hide | ((feat_row == 3) & (w >= 4))
                QXT32[j] = jnp.where(hide, -BIG, 0.0).astype(BF16)

    def l2_copy(j):
        return pltpu.make_async_remote_copy(
            src_ref=inbuf.at[2 * j, :, pl.ds(0, 64), :], dst_ref=kv2.at[j, 1],
            send_sem=l2_ss.at[j], recv_sem=l2_rs.at[j], device_id={"seq": pair}, device_id_type=MESH)

    def l8_copy(j, k):
        return pltpu.make_async_remote_copy(
            src_ref=inbuf.at[2 * j, :, pl.ds(0, 16), :], dst_ref=kv8.at[j, 8 - k],
            send_sem=l8_ss.at[7 * j + k - 1], recv_sem=l8_rs.at[7 * j + k - 1],
            device_id={"seq": oct_peer(k)}, device_id_type=MESH)

    def l32_copy(j, k):
        return pltpu.make_async_remote_copy(
            src_ref=kv32.at[j, 0], dst_ref=kv32.at[j, 16 - k],
            send_sem=l32_ss.at[15 * j + k - 1], recv_sem=l32_rs.at[15 * j + k - 1],
            device_id={"seq": plane_peer(k)}, device_id_type=MESH)

    def pick(j):
        row, col = iota((32, 128), 0), iota((32, 128), 1)
        return (col == (row >> 2) * 16 + (row & 3) + 4 * j).astype(F32).astype(BF16)

    def start_levels(j):
        l2_copy(j).start()
        for k in range(1, 8):
            l8_copy(j, k).start()
        if j == 0:
            for k in range(NH):
                zin_copy(k).wait_recv()
        kv32[j, 0, 0] = nn(pick(0), inbuf[2 * j, :, 0:16].reshape(128, 128)).astype(BF16)
        kv32[j, 0, 1] = nn(pick(j), zin[...].reshape(128, 128)).astype(BF16)
        for k in range(1, 16):
            l32_copy(j, k).start()
        kv2[j, 0] = inbuf[2 * j, :, 0:64]
        kv8[j, 0] = inbuf[2 * j, :, 0:16]

    def prepare(level, j, load):
        for c in range(8):
            rows = slice(c * 128, c * 128 + 128)
            kv = load(c).astype(F32)
            KX[level, j, rows] = jnp.where(low, kv, KX[level, j, rows].astype(F32)).astype(BF16)
            KVT[level, j, :, rows] = kv.T.astype(BF16)

    def natural(level, j):
        ref = (inbuf.at[2 * j], kv2.at[j], kv8.at[j], kv32.at[j])[level]
        return ref[...].reshape(1024, 128)

    def prepare_queries(j, part):
        x = inbuf.at[2 * j + 1, :, pl.ds(64 * part, 64)]
        QG[0:128] = x[:, 0:16].reshape(128, 128)
        QG[128:512] = x[:, 16:64].reshape(384, 128)
        for i in range(4):
            c = 4 * part + i
            rows = slice(c * 128, c * 128 + 128)
            qd = QG[i * 128:i * 128 + 128].astype(F32)
            query, up = qd * 0.125, jnp.where(low, 0.0, qd)
            query_t = query.T
            QM[j, rows] = jnp.where(low, query, 0.0).astype(BF16)
            DOM[j, rows] = up.astype(BF16)
            DOT[j, c] = up.T.astype(BF16)
            QXT[j, c] = jnp.where(row128 < 64, query_t, QXT[j, c].astype(F32)).astype(BF16)
            if c == 0:
                QXT32[j] = jnp.where(row128 < 64, query_t, QXT32[j].astype(F32)).astype(BF16)

    def wide(ref, j, b):
        return jnp.concatenate([ref[j, 4 * b + i] for i in range(4)], axis=1)

    def forward(level, j, qxt, weights):
        sc = nn(KX[level, j], qxt)
        m = jnp.max(sc, axis=0, keepdims=True)
        w = jnp.exp(sc - m)
        weights[...] = w
        total = jnp.sum(w, axis=0, keepdims=True)
        o = nn(KVT[level, j, 64:128], w.astype(BF16))
        return m, total, o

    def backward(level, j, weights, factor, delta, dot_t, rows):
        p = weights[...] * factor
        dp = nn(natural(level, j), dot_t)
        ds = (p * (dp - delta)).astype(BF16)
        return nn(ds, QM[j, rows]) + nn(p.astype(BF16), DOM[j, rows]), nn(KVT[level, j, 0:64], ds)

    def out_copy(i, src, row, n, k):
        return pltpu.make_async_remote_copy(
            src_ref=src.at[head_peer(k)], dst_ref=out_ref.at[h, pl.ds(row, n)],
            send_sem=out_ss.at[i * 7 + k - 1], recv_sem=out_rs.at[i * 7 + k - 1],
            device_id={"head": head_peer(k)}, device_id_type=MESH)

    def out_local(i, src, row, n):
        return pltpu.make_async_copy(src.at[h], out_ref.at[h, pl.ds(row, n)], out_loc.at[i])

    def og_part(row, n):
        return og.at[:, pl.ds(row, n)]

    parts = []
    for j in range(2):
        parts += [(ROW_Q[j][0], 64), (ROW_Q[j][1], 64), (ROW_KV[j] + 16, 48), (ROW_KV[j], 16),
                  (ROW_KV[j] + 64, 64)]

    def start_out(i):
        row, n = parts[i]
        for k in range(1, NH):
            out_copy(i, og_part(row, n), row, n, k).start()
        out_local(i, og_part(row, n), row, n).start()

    def tz_copy(k):
        return pltpu.make_async_remote_copy(
            src_ref=og.at[head_peer(k), pl.ds(ROW_TZ, 16)], dst_ref=out_ref.at[h, pl.ds(ROW_TZ, 16)],
            send_sem=tz_ss.at[k], recv_sem=tz_rs.at[k],
            device_id={"seq": zpeer, "head": head_peer(k)}, device_id_type=MESH)

    def send_rows(i, top, bottom):
        row = parts[i][0]
        both = jnp.concatenate([top, bottom], axis=0).T.astype(BF16)
        og[:, row:row + 16] = both[0:128].reshape(8, 16, 128)
        og[:, row + 16:row + 64] = both[128:512].reshape(8, 48, 128)
        start_out(i)

    def g32_copy(j, k):
        return pltpu.make_async_remote_copy(
            src_ref=g32.at[j, k], dst_ref=r32.at[j, 16 - k],
            send_sem=l32_ss.at[29 + 15 * j + k], recv_sem=l32_rs.at[29 + 15 * j + k],
            device_id={"seq": plane_peer(k)}, device_id_type=MESH)

    def g8_copy(j, k):
        return pltpu.make_async_remote_copy(
            src_ref=g8.at[j, k], dst_ref=r8.at[j, 8 - k],
            send_sem=l8_ss.at[13 + 7 * j + k], recv_sem=l8_rs.at[13 + 7 * j + k],
            device_id={"seq": oct_peer(k)}, device_id_type=MESH)

    def g2_copy(j):
        return pltpu.make_async_remote_copy(
            src_ref=g2.at[j], dst_ref=r2.at[j], send_sem=l2_ss.at[2 + j], recv_sem=l2_rs.at[2 + j],
            device_id={"seq": pair}, device_id_type=MESH)

    def put(j):
        row, col = iota((128, 32), 0), iota((128, 32), 1)
        return (row == (col >> 2) * 16 + (col & 3) + 4 * j).astype(F32).astype(BF16)

    def spread(j, x):
        hi = x.astype(BF16)
        return nn(put(j), hi) + nn(put(j), (x - hi.astype(F32)).astype(BF16))

    def send_keys(j):
        g2_copy(j).wait()
        for b in range(8):
            t2 = ACC[1, j, b * 64 + 16:b * 64 + 64] + r2[j, b, 16:64].astype(F32)
            own = ACC[0, j, b * 128 + 16:b * 128 + 64]
            og[b, ROW_KV[j] + 16:ROW_KV[j] + 64] = (own + t2).astype(BF16)
        start_out(5 * j + 2)

    def send_other_keys(j):
        for b in range(8):
            og[b, ROW_KV[j] + 64:ROW_KV[j] + 128] = ACC[0, j, b * 128 + 64:b * 128 + 128].astype(BF16)
        start_out(5 * j + 4)

    def sum_plane(j):
        for k in range(1, 16):
            g32_copy(j, k).wait()
        total = ACC[3, j, 0:64]
        for m in range(1, 16):
            total += r32[j, m].reshape(64, 128).astype(F32)
        ACC[3, j, 0:64] = total

    def send_tiles(j):
        for k in range(1, 8):
            g8_copy(j, k).wait()
        t8 = ACC[2, j, 0:128] + spread(0, ACC[3, j, 0:32])
        for m in range(1, 8):
            t8 += r8[j, m].astype(F32)
        for b in range(8):
            t2 = ACC[1, j, b * 64:b * 64 + 16] + r2[j, b, 0:16].astype(F32)
            own = ACC[0, j, b * 128:b * 128 + 16]
            og[b, ROW_KV[j]:ROW_KV[j] + 16] = (own + t2 + t8[b * 16:b * 16 + 16]).astype(BF16)
        start_out(5 * j + 3)

    def send_plane():
        both = spread(0, ACC[3, 0, 32:64]) + spread(1, ACC[3, 1, 32:64])
        og[:, ROW_TZ:ROW_TZ + 16] = both.astype(BF16).reshape(8, 16, 128)
        for k in range(NH):
            tz_copy(k).start()

    def prepare_local(j):
        prepare(0, j, lambda c: inbuf[2 * j, c])

    def row_delta(j, part, o):
        return jnp.sum(wide(DOT, j, part)[64:128].astype(F32) * o, axis=0, keepdims=True)

    def attend_other(j):
        prepare_queries(j, 1)
        _, total, o = forward(0, j, wide(QXT, j, 1), WB)
        factor = 1.0 / total
        o = o * factor
        acc, dq = backward(0, j, WB, factor, row_delta(j, 1, o), wide(DOT, j, 1), slice(512, 1024))
        ACC[0, j] = acc if j == 0 else ACC[0, j] + acc
        send_rows(5 * j + 1, dq * 0.125, o)

    def attend_own(j, before):
        m1, l1, o1 = forward(0, j, wide(QXT, j, 0), W1)
        before()
        l2_copy(j).wait()
        prepare(1, j, lambda c: kv2[j, c // 4, c % 4 * 2:c % 4 * 2 + 2].reshape(128, 128))
        m2, l2, o2 = forward(1, j, wide(QXT, j, 0), W2)
        for k in range(1, 8):
            l8_copy(j, k).wait()
        prepare(2, j, lambda c: kv8[j, c].reshape(128, 128))
        m3, l3, o3 = forward(2, j, QXT[j, 0], W8)
        for k in range(1, 16):
            l32_copy(j, k).wait()
        prepare(3, j, lambda c: kv32[j, 2 * c:2 * c + 2].reshape(128, 128))
        m4, l4, o4 = forward(3, j, QXT32[j], W32)

        def on_first(x, f):
            return jnp.concatenate([f(x[:, 0:128]), x[:, 128:512]], axis=1)

        top = on_first(jnp.maximum(m1, m2), lambda x: jnp.maximum(x, jnp.maximum(m3, m4)))
        e1, e2 = jnp.exp(m1 - top), jnp.exp(m2 - top)
        e3, e4 = jnp.exp(m3 - top[:, 0:128]), jnp.exp(m4 - top[:, 0:128])
        factor = 1.0 / on_first(l1 * e1 + l2 * e2, lambda x: x + l3 * e3 + l4 * e4)
        o = on_first(o1 * e1 + o2 * e2, lambda x: x + o3 * e3 + o4 * e4) * factor
        delta = row_delta(j, 0, o)
        short = factor[:, 0:128], delta[:, 0:128]

        ACC[1, j], dq2 = backward(1, j, W2, e2 * factor, delta, wide(DOT, j, 0), slice(0, 512))
        g2[j] = ACC[1, j, 512:1024].reshape(8, 64, 128).astype(BF16)
        g2_copy(j).start()
        ACC[3, j], dq4 = backward(3, j, W32, e4 * short[0], short[1], DOT[j, 0], slice(0, 128))
        g32[j] = ACC[3, j].reshape(16, 2, 32, 128).astype(BF16)
        for k in range(1, 16):
            g32_copy(j, k).start()
        ACC[2, j], dq3 = backward(2, j, W8, e3 * short[0], short[1], DOT[j, 0], slice(0, 128))
        g8[j] = ACC[2, j].reshape(8, 128, 128).astype(BF16)
        for k in range(1, 8):
            g8_copy(j, k).start()
        acc, dq1 = backward(0, j, W1, e1 * factor, delta, wide(DOT, j, 0), slice(0, 512))
        ACC[0, j] = acc if j == 1 else ACC[0, j] + acc
        send_rows(5 * j, on_first(dq1 + dq2, lambda x: x + dq3 + dq4) * 0.125, o)

    wait_in(0)
    start_levels(0)
    wait_in(1)
    start_levels(1)
    wait_in(2)
    prepare_local(0)
    wait_in(3)
    attend_other(0)
    wait_in(4)
    prepare_queries(0, 0)
    attend_own(0, lambda: None)
    send_other_keys(0)
    wait_in(5)
    prepare_local(1)
    wait_in(6)
    prepare_queries(1, 0)
    attend_own(1, lambda: send_keys(0))
    wait_in(7)
    attend_other(1)
    send_other_keys(1)
    sum_plane(0)
    send_tiles(0)
    send_keys(1)
    sum_plane(1)
    send_plane()
    send_tiles(1)

    for i in range(8):
        for k in range(1, NH):
            in_copy(i, k).wait_send()
    for k in range(NH):
        zin_copy(k).wait_send()
        tz_copy(k).wait()
    for i, (row, n) in enumerate(parts):
        for k in range(1, NH):
            out_copy(i, og_part(row, n), row, n, k).wait()
        out_local(i, og_part(row, n), row, n).wait()


def restore_kernel(packed_ref, a_ref, q_ref, k_ref, v_ref):
    low = iota((128, 128), 1) < 64
    first4 = iota((16, 128), 0) < 4
    for g in range(NH):
        rho = iota((NB, NB), 1)
        mat = (iota((NB, NB), 0) == token_of(rho >> 6, rho & 63, g)).astype(F32).astype(BF16)
        cols = []
        for j in range(2):
            both = [packed_ref[g, row:row + 64] for row in ROW_Q[j]]
            cols.append(jnp.concatenate(both[::-1] if j else both, axis=0))
        for j in range(2):
            plane = packed_ref[g, ROW_TZ:ROW_TZ + 16].astype(F32)
            plane = jnp.where(first4, pltpu.roll(plane, 12, 0) if j else plane, 0.0)
            tile = packed_ref[g, ROW_KV[j]:ROW_KV[j] + 16].astype(F32) + plane
            own = [tile.astype(BF16), packed_ref[g, ROW_KV[j] + 16:ROW_KV[j] + 64]]
            other = [packed_ref[g, ROW_KV[j] + 64:ROW_KV[j] + 128]]
            cols.append(jnp.concatenate(other + own if j else own + other, axis=0))
        res = nn(mat, jnp.concatenate(cols, axis=1))
        here = slice(g * 128, g * 128 + 128)
        for first, second, at in ((q_ref, a_ref, 0), (k_ref, v_ref, 256)):
            x, y = res[:, at:at + 128], res[:, at + 128:at + 256]
            first[:, here] = jnp.where(low, x, pltpu.roll(y, 64, 1)).astype(BF16)
            second[:, here] = jnp.where(low, pltpu.roll(x, 64, 1), y).astype(BF16)


def body(queries, keys, values, grad_out, doc_ids):
    vmem = pl.BlockSpec(memory_space=pltpu.VMEM)
    dma = pltpu.SemaphoreType.DMA
    packed = pl.pallas_call(
        attend_kernel,
        out_shape=jax.ShapeDtypeStruct((NH, ROWS, 128), BF16),
        in_specs=[pl.BlockSpec(memory_space=pl.ANY)] * 5,
        out_specs=pl.BlockSpec(memory_space=pl.ANY),
        scratch_shapes=[pltpu.VMEM(queries.shape, BF16)] * 4 + [
            pltpu.VMEM((256, 128), I32),
            pltpu.VMEM((4, NH, NB, 128), BF16),
            pltpu.VMEM((NH, 16, 128), BF16),
            pltpu.VMEM((4, NH, NB, 128), BF16),
            pltpu.VMEM((NH, 16, 128), BF16),
            pltpu.VMEM((2, 2, 8, 64, 128), BF16),
            pltpu.VMEM((2, 8, 8, 16, 128), BF16),
            pltpu.VMEM((2, 16, 2, 32, 128), BF16),
            pltpu.VMEM((4, 2, 1024, 128), BF16),
            pltpu.VMEM((4, 2, 128, 1024), BF16),
            pltpu.VMEM((512, 128), BF16),
            pltpu.VMEM((2, 8, 128, 128), BF16),
            pltpu.VMEM((2, 128, 128), BF16),
            pltpu.VMEM((2, 1024, 128), BF16),
            pltpu.VMEM((2, 1024, 128), BF16),
            pltpu.VMEM((2, 8, 128, 128), BF16),
            pltpu.VMEM((1024, 512), F32),
            pltpu.VMEM((1024, 512), F32),
            pltpu.VMEM((1024, 512), F32),
            pltpu.VMEM((1024, 128), F32),
            pltpu.VMEM((1024, 128), F32),
            pltpu.VMEM((4, 2, 1024, 128), F32),
            pltpu.VMEM((2, 8, 64, 128), BF16),
            pltpu.VMEM((2, 8, 64, 128), BF16),
            pltpu.VMEM((2, 8, 128, 128), BF16),
            pltpu.VMEM((2, 8, 128, 128), BF16),
            pltpu.VMEM((2, 16, 2, 32, 128), BF16),
            pltpu.VMEM((2, 16, 2, 32, 128), BF16),
            pltpu.VMEM((NH, ROWS, 128), BF16),
            dma((5,)), dma((56,)), dma((56,)), dma((8,)), dma((8,)), dma((8,)),
            dma((4,)), dma((4,)), dma((28,)), dma((28,)), dma((60,)), dma((60,)),
            dma((70,)), dma((70,)), dma((8,)), dma((8,)), dma((10,)),
        ],
        compiler_params=pltpu.CompilerParams(
            collective_id=0, has_side_effects=True, vmem_limit_bytes=56 * 1024 * 1024),
        name="attend",
    )(queries, keys, values, grad_out, doc_ids.reshape(256, 128))
    shape = jax.ShapeDtypeStruct(queries.shape, BF16)
    return pl.pallas_call(
        restore_kernel,
        out_shape=(shape, shape, shape, shape),
        in_specs=[vmem],
        out_specs=(vmem, vmem, vmem, vmem),
        compiler_params=pltpu.CompilerParams(vmem_limit_bytes=32 * 1024 * 1024),
        name="restore",
    )(packed)


def solution(mesh):
    spec = P(("seq", "head"), None)
    return jax.shard_map(
        body, mesh=mesh, in_specs=(spec, spec, spec, spec, P()), out_specs=(spec, spec, spec, spec), check_vma=False)
```

```python
import jax
import jax.numpy as jnp
from jax import lax
from jax.experimental import pallas as pl
from jax.experimental.pallas import tpu as pltpu
from jax.sharding import PartitionSpec as P

F32 = jnp.float32
BF16 = jnp.bfloat16
I32 = jnp.int32
BIG = 1e30
NH = 8
NB = 128
MESH = pl.DeviceIdType.MESH
ROW_Q, ROW_KV, ROW_TZ, ROWS = ((0, 64), (128, 192)), (256, 384), 512, 528


def iota(shape, dim):
    return lax.broadcasted_iota(I32, shape, dim)


def token_of(parity, w, h):
    t, u, a = (w >> 4) & 3, (w >> 2) & 3, w & 3
    return a * 32 + parity + 2 * ((h + t) & 3) + 8 * ((h // 4 + u) & 3)


def nn(a, b):
    return lax.dot_general(a, b, (((1,), (0,)), ((), ())), preferred_element_type=F32)


def attend_kernel(
    q_hbm, k_hbm, v_hbm, do_hbm, docs_hbm, out_ref,
    q_ref, k_ref, v_ref, do_ref, docs_ref,
    send, zsend, inbuf, zin, kv2, kv8, kv32, KX, KVT, QG, QXT, QXT32, QM, DOM, DOT,
    WB, W1, W2, W8, W32, ACC, g2, r2, g8, r8, g32, r32, og,
    load_s, in_ss, in_rs, zin_ss, zin_rs, loc_s, l2_ss, l2_rs, l8_ss, l8_rs, l32_ss, l32_rs,
    out_ss, out_rs, tz_ss, tz_rs, out_loc,
):
    h = lax.axis_index("head")
    s = lax.axis_index("seq")
    pair = s + 1 - 2 * (s % 2)
    base8 = (s // 8) * 8
    base16 = (s // 16) * 16
    zpeer = (s + 16) % 32

    def plane_peer(k):
        return base16 + (s - base16 + k) % 16

    def oct_peer(k):
        return base8 + (s - base8 + k) % 8

    def head_peer(k):
        return (h + k) % NH

    pairs = ((k_hbm, k_ref), (v_hbm, v_ref), (q_hbm, q_ref), (do_hbm, do_ref), (docs_hbm, docs_ref))
    loads = [pltpu.make_async_copy(a, b, load_s.at[i]) for i, (a, b) in enumerate(pairs)]
    for load in loads:
        load.start()

    barrier = pltpu.get_barrier_semaphore()
    for k in range(1, NH):
        pl.semaphore_signal(barrier, inc=1, device_id={"head": head_peer(k)}, device_id_type=MESH)
    for k in range(1, 16):
        pl.semaphore_signal(barrier, inc=1, device_id={"seq": plane_peer(k)}, device_id_type=MESH)
    for k in range(NH):
        pl.semaphore_signal(barrier, inc=1, device_id={"seq": zpeer, "head": head_peer(k)}, device_id_type=MESH)

    lane128 = iota((128, 128), 1)
    row128 = iota((128, 128), 0)
    low = lane128 < 64

    def permute_two(first, a_ref, b_ref):
        for g in range(NH):
            mat = (lane128 == token_of(row128 >> 6, row128 & 63, g)).astype(F32).astype(BF16)
            cols = slice(g * 128, g * 128 + 128)
            res = nn(mat, jnp.concatenate([a_ref[:, cols], b_ref[:, cols]], axis=1))
            a, b = res[:, 0:128], res[:, 128:256]
            one = jnp.where(low, a, pltpu.roll(b, 64, 1))
            other = jnp.where(low, pltpu.roll(a, 64, 1), b)
            send[first, g] = one.astype(BF16)
            send[first + 2, g, 0:64] = other[64:128].astype(BF16)
            send[first + 2, g, 64:128] = other[0:64].astype(BF16)
            if first == 0:
                zsend[g] = jnp.where(row128[0:16] < 4, one[0:16], pltpu.roll(other[64:80], 4, 0)).astype(BF16)

    messages = tuple((t, row, 64) for t, row in (
        (0, 0), (2, 0), (0, 64), (1, 64), (1, 0), (2, 64), (3, 0), (3, 64)))

    def in_copy(i, k):
        t, row, n = messages[i]
        return pltpu.make_async_remote_copy(
            src_ref=send.at[t, head_peer(k), pl.ds(row, n)], dst_ref=inbuf.at[t, h, pl.ds(row, n)],
            send_sem=in_ss.at[i * 7 + k - 1], recv_sem=in_rs.at[i * 7 + k - 1],
            device_id={"head": head_peer(k)}, device_id_type=MESH)

    def in_local(i):
        t, row, n = messages[i]
        return pltpu.make_async_copy(
            send.at[t, h, pl.ds(row, n)], inbuf.at[t, h, pl.ds(row, n)], loc_s.at[i])

    def start_in(i):
        for k in range(1, NH):
            in_copy(i, k).start()
        in_local(i).start()

    def wait_in(i):
        for k in range(1, NH):
            in_copy(i, k).wait_recv()
        in_local(i).wait()

    def zin_copy(k):
        return pltpu.make_async_remote_copy(
            src_ref=zsend.at[head_peer(k)], dst_ref=zin.at[h],
            send_sem=zin_ss.at[k], recv_sem=zin_rs.at[k],
            device_id={"seq": zpeer, "head": head_peer(k)}, device_id_type=MESH)

    loads[0].wait()
    loads[1].wait()
    permute_two(0, k_ref, v_ref)
    pl.semaphore_wait(barrier, 30)
    for k in range(NH):
        zin_copy(k).start()
    for i in range(3):
        start_in(i)
    loads[2].wait()
    loads[3].wait()
    permute_two(1, q_ref, do_ref)
    for i in range(3, 8):
        start_in(i)
    loads[4].wait()

    docs = docs_ref[...]

    def count(limit):
        c = jnp.sum((docs < limit).astype(F32), axis=0, keepdims=True)
        return jnp.sum(c, axis=1, keepdims=True).astype(I32)

    bound1, bound2 = count(1), count(2)

    def doc_of(pos):
        return (pos >= bound1).astype(I32) + (pos >= bound2).astype(I32)

    def key_place(level, c):
        r = row128 + c * 128
        if level == 0:
            return s, r >> 7, r & 127
        if level == 1:
            return jnp.where((r >> 9) == 0, s, pair), (r >> 6) & 7, r & 63
        if level == 2:
            return base8 + ((s + (r >> 7)) & 7), (r >> 4) & 7, r & 15
        plane = jnp.where(((r >> 5) & 1) == 0, base16, 16 - base16)
        return plane + ((s + (r >> 6)) & 15), (r >> 2) & 7, r & 3

    def fill_features(c, carry):
        for level in range(4):
            seqs, src, w = key_place(level, c)
            start = seqs * 1024 + src * 128
            for j in range(2):
                parity = j ^ (w >> 6)
                doc = doc_of(start + token_of(parity, w & 63, h))
                hot = (lane128 - 64 == doc) | (lane128 == 67)
                KX[level, j, pl.ds(c * 128, 128)] = jnp.where(hot, 1.0, 0.0).astype(BF16)
        return carry

    lax.fori_loop(0, 8, fill_features, 0)

    feat_row = row128 - 64
    for c in range(8):
        if c % 4 == 0:
            src, w = lane128 >> 4, lane128 & 15
        else:
            i = lane128 + (c % 4 - 1) * 128
            src = (i * 1366) >> 16
            w = 16 + i - src * 48
        w = w + 64 * (c // 4)
        for j in range(2):
            parity = j ^ (w >> 6)
            doc = doc_of(s * 1024 + src * 128 + token_of(parity, w & 63, h))
            hide = (feat_row >= 0) & (feat_row < 3) & (feat_row != doc)
            QXT[j, c] = jnp.where(hide, -BIG, 0.0).astype(BF16)
            if c == 0:
                hide = hide | ((feat_row == 3) & (w >= 4))
                QXT32[j] = jnp.where(hide, -BIG, 0.0).astype(BF16)

    def l2_copy(j):
        return pltpu.make_async_remote_copy(
            src_ref=inbuf.at[2 * j, :, pl.ds(0, 64), :], dst_ref=kv2.at[j, 1],
            send_sem=l2_ss.at[j], recv_sem=l2_rs.at[j], device_id={"seq": pair}, device_id_type=MESH)

    def l8_copy(j, k):
        return pltpu.make_async_remote_copy(
            src_ref=inbuf.at[2 * j, :, pl.ds(0, 16), :], dst_ref=kv8.at[j, 8 - k],
            send_sem=l8_ss.at[7 * j + k - 1], recv_sem=l8_rs.at[7 * j + k - 1],
            device_id={"seq": oct_peer(k)}, device_id_type=MESH)

    def l32_copy(j, k):
        return pltpu.make_async_remote_copy(
            src_ref=kv32.at[j, 0], dst_ref=kv32.at[j, 16 - k],
            send_sem=l32_ss.at[15 * j + k - 1], recv_sem=l32_rs.at[15 * j + k - 1],
            device_id={"seq": plane_peer(k)}, device_id_type=MESH)

    def pick(j):
        row, col = iota((32, 128), 0), iota((32, 128), 1)
        return (col == (row >> 2) * 16 + (row & 3) + 4 * j).astype(F32).astype(BF16)

    def start_levels(j):
        l2_copy(j).start()
        for k in range(1, 8):
            l8_copy(j, k).start()
        if j == 0:
            for k in range(NH):
                zin_copy(k).wait_recv()
        kv32[j, 0, 0] = nn(pick(0), inbuf[2 * j, :, 0:16].reshape(128, 128)).astype(BF16)
        kv32[j, 0, 1] = nn(pick(j), zin[...].reshape(128, 128)).astype(BF16)
        for k in range(1, 16):
            l32_copy(j, k).start()
        kv2[j, 0] = inbuf[2 * j, :, 0:64]
        kv8[j, 0] = inbuf[2 * j, :, 0:16]

    def prepare(level, j, load):
        for c in range(8):
            rows = slice(c * 128, c * 128 + 128)
            kv = load(c).astype(F32)
            KX[level, j, rows] = jnp.where(low, kv, KX[level, j, rows].astype(F32)).astype(BF16)
            KVT[level, j, :, rows] = kv.T.astype(BF16)

    def natural(level, j):
        ref = (inbuf.at[2 * j], kv2.at[j], kv8.at[j], kv32.at[j])[level]
        return ref[...].reshape(1024, 128)

    def prepare_queries(j, part):
        x = inbuf.at[2 * j + 1, :, pl.ds(64 * part, 64)]
        QG[0:128] = x[:, 0:16].reshape(128, 128)
        QG[128:512] = x[:, 16:64].reshape(384, 128)
        for i in range(4):
            c = 4 * part + i
            rows = slice(c * 128, c * 128 + 128)
            qd = QG[i * 128:i * 128 + 128].astype(F32)
            query, up = qd * 0.125, jnp.where(low, 0.0, qd)
            query_t = query.T
            QM[j, rows] = jnp.where(low, query, 0.0).astype(BF16)
            DOM[j, rows] = up.astype(BF16)
            DOT[j, c] = up.T.astype(BF16)
            QXT[j, c] = jnp.where(row128 < 64, query_t, QXT[j, c].astype(F32)).astype(BF16)
            if c == 0:
                QXT32[j] = jnp.where(row128 < 64, query_t, QXT32[j].astype(F32)).astype(BF16)

    def wide(ref, j, b):
        return jnp.concatenate([ref[j, 4 * b + i] for i in range(4)], axis=1)

    def forward(level, j, qxt, weights):
        sc = nn(KX[level, j], qxt)
        m = jnp.max(sc, axis=0, keepdims=True)
        w = jnp.exp(sc - m)
        weights[...] = w
        total = jnp.sum(w, axis=0, keepdims=True)
        o = nn(KVT[level, j, 64:128], w.astype(BF16))
        return m, total, o

    def backward(level, j, weights, factor, delta, dot_t, rows):
        p = weights[...] * factor
        dp = nn(natural(level, j), dot_t)
        ds = (p * (dp - delta)).astype(BF16)
        return nn(ds, QM[j, rows]) + nn(p.astype(BF16), DOM[j, rows]), nn(KVT[level, j, 0:64], ds)

    def out_copy(i, src, row, n, k):
        return pltpu.make_async_remote_copy(
            src_ref=src.at[head_peer(k)], dst_ref=out_ref.at[h, pl.ds(row, n)],
            send_sem=out_ss.at[i * 7 + k - 1], recv_sem=out_rs.at[i * 7 + k - 1],
            device_id={"head": head_peer(k)}, device_id_type=MESH)

    def out_local(i, src, row, n):
        return pltpu.make_async_copy(src.at[h], out_ref.at[h, pl.ds(row, n)], out_loc.at[i])

    def og_part(row, n):
        return og.at[:, pl.ds(row, n)]

    parts = []
    for j in range(2):
        parts += [(ROW_Q[j][0], 64), (ROW_Q[j][1], 64), (ROW_KV[j] + 16, 48), (ROW_KV[j], 16),
                  (ROW_KV[j] + 64, 64)]

    def start_out(i):
        row, n = parts[i]
        for k in range(1, NH):
            out_copy(i, og_part(row, n), row, n, k).start()
        out_local(i, og_part(row, n), row, n).start()

    def tz_copy(k):
        return pltpu.make_async_remote_copy(
            src_ref=og.at[head_peer(k), pl.ds(ROW_TZ, 16)], dst_ref=out_ref.at[h, pl.ds(ROW_TZ, 16)],
            send_sem=tz_ss.at[k], recv_sem=tz_rs.at[k],
            device_id={"seq": zpeer, "head": head_peer(k)}, device_id_type=MESH)

    def send_rows(i, top, bottom):
        row = parts[i][0]
        both = jnp.concatenate([top, bottom], axis=0).T.astype(BF16)
        og[:, row:row + 16] = both[0:128].reshape(8, 16, 128)
        og[:, row + 16:row + 64] = both[128:512].reshape(8, 48, 128)
        start_out(i)

    def g32_copy(j, k):
        return pltpu.make_async_remote_copy(
            src_ref=g32.at[j, k], dst_ref=r32.at[j, 16 - k],
            send_sem=l32_ss.at[29 + 15 * j + k], recv_sem=l32_rs.at[29 + 15 * j + k],
            device_id={"seq": plane_peer(k)}, device_id_type=MESH)

    def g8_copy(j, k):
        return pltpu.make_async_remote_copy(
            src_ref=g8.at[j, k], dst_ref=r8.at[j, 8 - k],
            send_sem=l8_ss.at[13 + 7 * j + k], recv_sem=l8_rs.at[13 + 7 * j + k],
            device_id={"seq": oct_peer(k)}, device_id_type=MESH)

    def g2_copy(j):
        return pltpu.make_async_remote_copy(
            src_ref=g2.at[j], dst_ref=r2.at[j], send_sem=l2_ss.at[2 + j], recv_sem=l2_rs.at[2 + j],
            device_id={"seq": pair}, device_id_type=MESH)

    def put(j):
        row, col = iota((128, 32), 0), iota((128, 32), 1)
        return (row == (col >> 2) * 16 + (col & 3) + 4 * j).astype(F32).astype(BF16)

    def spread(j, x):
        hi = x.astype(BF16)
        return nn(put(j), hi) + nn(put(j), (x - hi.astype(F32)).astype(BF16))

    def send_keys(j):
        g2_copy(j).wait()
        for b in range(8):
            t2 = ACC[1, j, b * 64 + 16:b * 64 + 64] + r2[j, b, 16:64].astype(F32)
            own = ACC[0, j, b * 128 + 16:b * 128 + 64]
            og[b, ROW_KV[j] + 16:ROW_KV[j] + 64] = (own + t2).astype(BF16)
        start_out(5 * j + 2)

    def send_other_keys(j):
        for b in range(8):
            og[b, ROW_KV[j] + 64:ROW_KV[j] + 128] = ACC[0, j, b * 128 + 64:b * 128 + 128].astype(BF16)
        start_out(5 * j + 4)

    def sum_plane(j):
        for k in range(1, 16):
            g32_copy(j, k).wait()
        total = ACC[3, j, 0:64]
        for m in range(1, 16):
            total += r32[j, m].reshape(64, 128).astype(F32)
        ACC[3, j, 0:64] = total

    def send_tiles(j):
        for k in range(1, 8):
            g8_copy(j, k).wait()
        t8 = ACC[2, j, 0:128] + spread(0, ACC[3, j, 0:32])
        for m in range(1, 8):
            t8 += r8[j, m].astype(F32)
        for b in range(8):
            t2 = ACC[1, j, b * 64:b * 64 + 16] + r2[j, b, 0:16].astype(F32)
            own = ACC[0, j, b * 128:b * 128 + 16]
            og[b, ROW_KV[j]:ROW_KV[j] + 16] = (own + t2 + t8[b * 16:b * 16 + 16]).astype(BF16)
        start_out(5 * j + 3)

    def send_plane():
        both = spread(0, ACC[3, 0, 32:64]) + spread(1, ACC[3, 1, 32:64])
        og[:, ROW_TZ:ROW_TZ + 16] = both.astype(BF16).reshape(8, 16, 128)
        for k in range(NH):
            tz_copy(k).start()

    def prepare_local(j):
        prepare(0, j, lambda c: inbuf[2 * j, c])

    def row_delta(j, part, o):
        return jnp.sum(wide(DOT, j, part)[64:128].astype(F32) * o, axis=0, keepdims=True)

    def attend_other(j):
        prepare_queries(j, 1)
        _, total, o = forward(0, j, wide(QXT, j, 1), WB)
        factor = 1.0 / total
        o = o * factor
        acc, dq = backward(0, j, WB, factor, row_delta(j, 1, o), wide(DOT, j, 1), slice(512, 1024))
        ACC[0, j] = acc if j == 0 else ACC[0, j] + acc
        send_rows(5 * j + 1, dq * 0.125, o)

    def attend_own(j, before):
        m1, l1, o1 = forward(0, j, wide(QXT, j, 0), W1)
        before()
        l2_copy(j).wait()
        prepare(1, j, lambda c: kv2[j, c // 4, c % 4 * 2:c % 4 * 2 + 2].reshape(128, 128))
        m2, l2, o2 = forward(1, j, wide(QXT, j, 0), W2)
        for k in range(1, 8):
            l8_copy(j, k).wait()
        prepare(2, j, lambda c: kv8[j, c].reshape(128, 128))
        m3, l3, o3 = forward(2, j, QXT[j, 0], W8)
        for k in range(1, 16):
            l32_copy(j, k).wait()
        prepare(3, j, lambda c: kv32[j, 2 * c:2 * c + 2].reshape(128, 128))
        m4, l4, o4 = forward(3, j, QXT32[j], W32)

        def on_first(x, f):
            return jnp.concatenate([f(x[:, 0:128]), x[:, 128:512]], axis=1)

        top = on_first(jnp.maximum(m1, m2), lambda x: jnp.maximum(x, jnp.maximum(m3, m4)))
        e1, e2 = jnp.exp(m1 - top), jnp.exp(m2 - top)
        e3, e4 = jnp.exp(m3 - top[:, 0:128]), jnp.exp(m4 - top[:, 0:128])
        factor = 1.0 / on_first(l1 * e1 + l2 * e2, lambda x: x + l3 * e3 + l4 * e4)
        o = on_first(o1 * e1 + o2 * e2, lambda x: x + o3 * e3 + o4 * e4) * factor
        delta = row_delta(j, 0, o)
        short = factor[:, 0:128], delta[:, 0:128]

        ACC[1, j], dq2 = backward(1, j, W2, e2 * factor, delta, wide(DOT, j, 0), slice(0, 512))
        g2[j] = ACC[1, j, 512:1024].reshape(8, 64, 128).astype(BF16)
        g2_copy(j).start()
        ACC[3, j], dq4 = backward(3, j, W32, e4 * short[0], short[1], DOT[j, 0], slice(0, 128))
        g32[j] = ACC[3, j].reshape(16, 2, 32, 128).astype(BF16)
        for k in range(1, 16):
            g32_copy(j, k).start()
        ACC[2, j], dq3 = backward(2, j, W8, e3 * short[0], short[1], DOT[j, 0], slice(0, 128))
        g8[j] = ACC[2, j].reshape(8, 128, 128).astype(BF16)
        for k in range(1, 8):
            g8_copy(j, k).start()
        acc, dq1 = backward(0, j, W1, e1 * factor, delta, wide(DOT, j, 0), slice(0, 512))
        ACC[0, j] = acc if j == 1 else ACC[0, j] + acc
        send_rows(5 * j, on_first(dq1 + dq2, lambda x: x + dq3 + dq4) * 0.125, o)

    wait_in(0)
    start_levels(0)
    wait_in(1)
    start_levels(1)
    wait_in(2)
    prepare_local(0)
    wait_in(3)
    attend_other(0)
    wait_in(4)
    prepare_queries(0, 0)
    attend_own(0, lambda: None)
    send_other_keys(0)
    wait_in(5)
    prepare_local(1)
    wait_in(6)
    prepare_queries(1, 0)
    attend_own(1, lambda: send_keys(0))
    sum_plane(0)
    send_tiles(0)
    wait_in(7)
    attend_other(1)
    send_other_keys(1)
    send_keys(1)
    sum_plane(1)
    send_plane()
    send_tiles(1)

    for i in range(8):
        for k in range(1, NH):
            in_copy(i, k).wait_send()
    for k in range(NH):
        zin_copy(k).wait_send()
        tz_copy(k).wait()
    for i, (row, n) in enumerate(parts):
        for k in range(1, NH):
            out_copy(i, og_part(row, n), row, n, k).wait()
        out_local(i, og_part(row, n), row, n).wait()


def restore_kernel(packed_ref, a_ref, q_ref, k_ref, v_ref):
    low = iota((128, 128), 1) < 64
    first4 = iota((16, 128), 0) < 4
    for g in range(NH):
        rho = iota((NB, NB), 1)
        mat = (iota((NB, NB), 0) == token_of(rho >> 6, rho & 63, g)).astype(F32).astype(BF16)
        cols = []
        for j in range(2):
            both = [packed_ref[g, row:row + 64] for row in ROW_Q[j]]
            cols.append(jnp.concatenate(both[::-1] if j else both, axis=0))
        for j in range(2):
            plane = packed_ref[g, ROW_TZ:ROW_TZ + 16].astype(F32)
            plane = jnp.where(first4, pltpu.roll(plane, 12, 0) if j else plane, 0.0)
            tile = packed_ref[g, ROW_KV[j]:ROW_KV[j] + 16].astype(F32) + plane
            own = [tile.astype(BF16), packed_ref[g, ROW_KV[j] + 16:ROW_KV[j] + 64]]
            other = [packed_ref[g, ROW_KV[j] + 64:ROW_KV[j] + 128]]
            cols.append(jnp.concatenate(other + own if j else own + other, axis=0))
        res = nn(mat, jnp.concatenate(cols, axis=1))
        here = slice(g * 128, g * 128 + 128)
        for first, second, at in ((q_ref, a_ref, 0), (k_ref, v_ref, 256)):
            x, y = res[:, at:at + 128], res[:, at + 128:at + 256]
            first[:, here] = jnp.where(low, x, pltpu.roll(y, 64, 1)).astype(BF16)
            second[:, here] = jnp.where(low, pltpu.roll(x, 64, 1), y).astype(BF16)


def body(queries, keys, values, grad_out, doc_ids):
    vmem = pl.BlockSpec(memory_space=pltpu.VMEM)
    dma = pltpu.SemaphoreType.DMA
    packed = pl.pallas_call(
        attend_kernel,
        out_shape=pltpu.VMEM((NH, ROWS, 128), BF16),
        in_specs=[pl.BlockSpec(memory_space=pl.ANY)] * 5,
        out_specs=vmem,
        scratch_shapes=[pltpu.VMEM(queries.shape, BF16)] * 4 + [
            pltpu.VMEM((256, 128), I32),
            pltpu.VMEM((4, NH, NB, 128), BF16),
            pltpu.VMEM((NH, 16, 128), BF16),
            pltpu.VMEM((4, NH, NB, 128), BF16),
            pltpu.VMEM((NH, 16, 128), BF16),
            pltpu.VMEM((2, 2, 8, 64, 128), BF16),
            pltpu.VMEM((2, 8, 8, 16, 128), BF16),
            pltpu.VMEM((2, 16, 2, 32, 128), BF16),
            pltpu.VMEM((4, 2, 1024, 128), BF16),
            pltpu.VMEM((4, 2, 128, 1024), BF16),
            pltpu.VMEM((512, 128), BF16),
            pltpu.VMEM((2, 8, 128, 128), BF16),
            pltpu.VMEM((2, 128, 128), BF16),
            pltpu.VMEM((2, 1024, 128), BF16),
            pltpu.VMEM((2, 1024, 128), BF16),
            pltpu.VMEM((2, 8, 128, 128), BF16),
            pltpu.VMEM((1024, 512), F32),
            pltpu.VMEM((1024, 512), F32),
            pltpu.VMEM((1024, 512), F32),
            pltpu.VMEM((1024, 128), F32),
            pltpu.VMEM((1024, 128), F32),
            pltpu.VMEM((4, 2, 1024, 128), F32),
            pltpu.VMEM((2, 8, 64, 128), BF16),
            pltpu.VMEM((2, 8, 64, 128), BF16),
            pltpu.VMEM((2, 8, 128, 128), BF16),
            pltpu.VMEM((2, 8, 128, 128), BF16),
            pltpu.VMEM((2, 16, 2, 32, 128), BF16),
            pltpu.VMEM((2, 16, 2, 32, 128), BF16),
            pltpu.VMEM((NH, ROWS, 128), BF16),
            dma((5,)), dma((56,)), dma((56,)), dma((8,)), dma((8,)), dma((8,)),
            dma((4,)), dma((4,)), dma((28,)), dma((28,)), dma((60,)), dma((60,)),
            dma((70,)), dma((70,)), dma((8,)), dma((8,)), dma((10,)),
        ],
        compiler_params=pltpu.CompilerParams(
            collective_id=0, has_side_effects=True, vmem_limit_bytes=56 * 1024 * 1024),
        name="attend",
    )(queries, keys, values, grad_out, doc_ids.reshape(256, 128))
    shape = jax.ShapeDtypeStruct(queries.shape, BF16)
    return pl.pallas_call(
        restore_kernel,
        out_shape=(shape, shape, shape, shape),
        in_specs=[vmem],
        out_specs=(vmem, vmem, vmem, vmem),
        compiler_params=pltpu.CompilerParams(vmem_limit_bytes=32 * 1024 * 1024),
        name="restore",
    )(packed)


def solution(mesh):
    spec = P(("seq", "head"), None)
    return jax.shard_map(
        body, mesh=mesh, in_specs=(spec, spec, spec, spec, P()), out_specs=(spec, spec, spec, spec), check_vma=False)
```

```python
import jax
import jax.numpy as jnp
from jax import lax
from jax.experimental import pallas as pl
from jax.experimental.pallas import tpu as pltpu
from jax.sharding import PartitionSpec as P

F32 = jnp.float32
BF16 = jnp.bfloat16
I32 = jnp.int32
BIG = 1e30
NH = 8
NB = 128
MESH = pl.DeviceIdType.MESH
ROW_Q, ROW_KV, ROW_TZ, ROWS = ((0, 64), (128, 192)), (256, 384), 512, 528


def iota(shape, dim):
    return lax.broadcasted_iota(I32, shape, dim)


def token_of(parity, w, h):
    t, u, a = (w >> 4) & 3, (w >> 2) & 3, w & 3
    return a * 32 + parity + 2 * ((h + t) & 3) + 8 * ((h // 4 + u) & 3)


def nn(a, b):
    return lax.dot_general(a, b, (((1,), (0,)), ((), ())), preferred_element_type=F32)


def attend_kernel(
    q_hbm, k_hbm, v_hbm, do_hbm, docs_hbm, out_ref,
    q_ref, k_ref, v_ref, do_ref, docs_ref,
    send, zsend, inbuf, zin, kv2, kv8, kv32, KX, KVT, QG, QXT, QXT32, QM, DOM, DOT,
    WB, W1, W2, W8, W32, ACC, g2, r2, g8, r8, g32, r32, og,
    load_s, in_ss, in_rs, zin_ss, zin_rs, loc_s, l2_ss, l2_rs, l8_ss, l8_rs, l32_ss, l32_rs,
    out_ss, out_rs, tz_ss, tz_rs, out_loc,
):
    h = lax.axis_index("head")
    s = lax.axis_index("seq")
    pair = s + 1 - 2 * (s % 2)
    base8 = (s // 8) * 8
    base16 = (s // 16) * 16
    zpeer = (s + 16) % 32

    def plane_peer(k):
        return base16 + (s - base16 + k) % 16

    def oct_peer(k):
        return base8 + (s - base8 + k) % 8

    def head_peer(k):
        return (h + k) % NH

    pairs = ((k_hbm, k_ref), (v_hbm, v_ref), (q_hbm, q_ref), (do_hbm, do_ref), (docs_hbm, docs_ref))
    loads = [pltpu.make_async_copy(a, b, load_s.at[i]) for i, (a, b) in enumerate(pairs)]
    for load in loads:
        load.start()

    barrier = pltpu.get_barrier_semaphore()
    for k in range(1, NH):
        pl.semaphore_signal(barrier, inc=1, device_id={"head": head_peer(k)}, device_id_type=MESH)
    for k in range(1, 16):
        pl.semaphore_signal(barrier, inc=1, device_id={"seq": plane_peer(k)}, device_id_type=MESH)
    for k in range(NH):
        pl.semaphore_signal(barrier, inc=1, device_id={"seq": zpeer, "head": head_peer(k)}, device_id_type=MESH)

    lane128 = iota((128, 128), 1)
    row128 = iota((128, 128), 0)
    low = lane128 < 64

    def permute_two(first, a_ref, b_ref):
        for g in range(NH):
            mat = (lane128 == token_of(row128 >> 6, row128 & 63, g)).astype(F32).astype(BF16)
            cols = slice(g * 128, g * 128 + 128)
            res = nn(mat, jnp.concatenate([a_ref[:, cols], b_ref[:, cols]], axis=1))
            a, b = res[:, 0:128], res[:, 128:256]
            one = jnp.where(low, a, pltpu.roll(b, 64, 1))
            other = jnp.where(low, pltpu.roll(a, 64, 1), b)
            send[first, g] = one.astype(BF16)
            send[first + 2, g, 0:64] = other[64:128].astype(BF16)
            send[first + 2, g, 64:128] = other[0:64].astype(BF16)
            if first == 0:
                zsend[g] = jnp.where(row128[0:16] < 4, one[0:16], pltpu.roll(other[64:80], 4, 0)).astype(BF16)

    messages = tuple((t, row, 64) for t, row in (
        (0, 0), (2, 0), (0, 64), (1, 64), (1, 0), (2, 64), (3, 0), (3, 64)))

    def in_copy(i, k):
        t, row, n = messages[i]
        return pltpu.make_async_remote_copy(
            src_ref=send.at[t, head_peer(k), pl.ds(row, n)], dst_ref=inbuf.at[t, h, pl.ds(row, n)],
            send_sem=in_ss.at[i * 7 + k - 1], recv_sem=in_rs.at[i * 7 + k - 1],
            device_id={"head": head_peer(k)}, device_id_type=MESH)

    def in_local(i):
        t, row, n = messages[i]
        return pltpu.make_async_copy(
            send.at[t, h, pl.ds(row, n)], inbuf.at[t, h, pl.ds(row, n)], loc_s.at[i])

    def start_in(i):
        for k in range(1, NH):
            in_copy(i, k).start()
        in_local(i).start()

    def wait_in(i):
        for k in range(1, NH):
            in_copy(i, k).wait_recv()
        in_local(i).wait()

    def zin_copy(k):
        return pltpu.make_async_remote_copy(
            src_ref=zsend.at[head_peer(k)], dst_ref=zin.at[h],
            send_sem=zin_ss.at[k], recv_sem=zin_rs.at[k],
            device_id={"seq": zpeer, "head": head_peer(k)}, device_id_type=MESH)

    loads[0].wait()
    loads[1].wait()
    permute_two(0, k_ref, v_ref)
    pl.semaphore_wait(barrier, 30)
    for k in range(NH):
        zin_copy(k).start()
    for i in range(3):
        start_in(i)
    loads[2].wait()
    loads[3].wait()
    permute_two(1, q_ref, do_ref)
    for i in range(3, 8):
        start_in(i)
    loads[4].wait()

    docs = docs_ref[...]

    def count(limit):
        c = jnp.sum((docs < limit).astype(F32), axis=0, keepdims=True)
        return jnp.sum(c, axis=1, keepdims=True).astype(I32)

    bound1, bound2 = count(1), count(2)

    def doc_of(pos):
        return (pos >= bound1).astype(I32) + (pos >= bound2).astype(I32)

    def key_place(level, c):
        r = row128 + c * 128
        if level == 0:
            return s, r >> 7, r & 127
        if level == 1:
            return jnp.where((r >> 9) == 0, s, pair), (r >> 6) & 7, r & 63
        if level == 2:
            return base8 + ((s + (r >> 7)) & 7), (r >> 4) & 7, r & 15
        plane = jnp.where(((r >> 5) & 1) == 0, base16, 16 - base16)
        return plane + ((s + (r >> 6)) & 15), (r >> 2) & 7, r & 3

    def fill_features(c, carry):
        for level in range(4):
            seqs, src, w = key_place(level, c)
            start = seqs * 1024 + src * 128
            for j in range(2):
                parity = j ^ (w >> 6)
                doc = doc_of(start + token_of(parity, w & 63, h))
                hot = (lane128 - 64 == doc) | (lane128 == 67)
                KX[level, j, pl.ds(c * 128, 128)] = jnp.where(hot, 1.0, 0.0).astype(BF16)
        return carry

    lax.fori_loop(0, 8, fill_features, 0)

    feat_row = row128 - 64
    for c in range(8):
        if c % 4 == 0:
            src, w = lane128 >> 4, lane128 & 15
        else:
            i = lane128 + (c % 4 - 1) * 128
            src = (i * 1366) >> 16
            w = 16 + i - src * 48
        w = w + 64 * (c // 4)
        for j in range(2):
            parity = j ^ (w >> 6)
            doc = doc_of(s * 1024 + src * 128 + token_of(parity, w & 63, h))
            hide = (feat_row >= 0) & (feat_row < 3) & (feat_row != doc)
            QXT[j, c] = jnp.where(hide, -BIG, 0.0).astype(BF16)
            if c == 0:
                hide = hide | ((feat_row == 3) & (w >= 4))
                QXT32[j] = jnp.where(hide, -BIG, 0.0).astype(BF16)

    def l2_copy(j):
        return pltpu.make_async_remote_copy(
            src_ref=inbuf.at[2 * j, :, pl.ds(0, 64), :], dst_ref=kv2.at[j, 1],
            send_sem=l2_ss.at[j], recv_sem=l2_rs.at[j], device_id={"seq": pair}, device_id_type=MESH)

    def l8_copy(j, k):
        return pltpu.make_async_remote_copy(
            src_ref=inbuf.at[2 * j, :, pl.ds(0, 16), :], dst_ref=kv8.at[j, 8 - k],
            send_sem=l8_ss.at[7 * j + k - 1], recv_sem=l8_rs.at[7 * j + k - 1],
            device_id={"seq": oct_peer(k)}, device_id_type=MESH)

    def l32_copy(j, k):
        return pltpu.make_async_remote_copy(
            src_ref=kv32.at[j, 0], dst_ref=kv32.at[j, 16 - k],
            send_sem=l32_ss.at[15 * j + k - 1], recv_sem=l32_rs.at[15 * j + k - 1],
            device_id={"seq": plane_peer(k)}, device_id_type=MESH)

    def pick(j):
        row, col = iota((32, 128), 0), iota((32, 128), 1)
        return (col == (row >> 2) * 16 + (row & 3) + 4 * j).astype(F32).astype(BF16)

    def start_levels(j):
        l2_copy(j).start()
        for k in range(1, 8):
            l8_copy(j, k).start()
        if j == 0:
            for k in range(NH):
                zin_copy(k).wait_recv()
        kv32[j, 0, 0] = nn(pick(0), inbuf[2 * j, :, 0:16].reshape(128, 128)).astype(BF16)
        kv32[j, 0, 1] = nn(pick(j), zin[...].reshape(128, 128)).astype(BF16)
        for k in range(1, 16):
            l32_copy(j, k).start()
        kv2[j, 0] = inbuf[2 * j, :, 0:64]
        kv8[j, 0] = inbuf[2 * j, :, 0:16]

    def prepare(level, j, load):
        for c in range(8):
            rows = slice(c * 128, c * 128 + 128)
            kv = load(c).astype(F32)
            KX[level, j, rows] = jnp.where(low, kv, KX[level, j, rows].astype(F32)).astype(BF16)
            KVT[level, j, :, rows] = kv.T.astype(BF16)

    def natural(level, j):
        ref = (inbuf.at[2 * j], kv2.at[j], kv8.at[j], kv32.at[j])[level]
        return ref[...].reshape(1024, 128)

    def prepare_queries(j, part):
        x = inbuf.at[2 * j + 1, :, pl.ds(64 * part, 64)]
        QG[0:128] = x[:, 0:16].reshape(128, 128)
        QG[128:512] = x[:, 16:64].reshape(384, 128)
        for i in range(4):
            c = 4 * part + i
            rows = slice(c * 128, c * 128 + 128)
            qd = QG[i * 128:i * 128 + 128].astype(F32)
            query, up = qd * 0.125, jnp.where(low, 0.0, qd)
            query_t = query.T
            QM[j, rows] = jnp.where(low, query, 0.0).astype(BF16)
            DOM[j, rows] = up.astype(BF16)
            DOT[j, c] = up.T.astype(BF16)
            QXT[j, c] = jnp.where(row128 < 64, query_t, QXT[j, c].astype(F32)).astype(BF16)
            if c == 0:
                QXT32[j] = jnp.where(row128 < 64, query_t, QXT32[j].astype(F32)).astype(BF16)

    def wide(ref, j, b):
        return jnp.concatenate([ref[j, 4 * b + i] for i in range(4)], axis=1)

    def forward(level, j, qxt, weights):
        sc = nn(KX[level, j], qxt)
        m = jnp.max(sc, axis=0, keepdims=True)
        w = jnp.exp(sc - m)
        weights[...] = w
        total = jnp.sum(w, axis=0, keepdims=True)
        o = nn(KVT[level, j, 64:128], w.astype(BF16))
        return m, total, o

    def backward(level, j, weights, factor, delta, dot_t, rows):
        p = weights[...] * factor
        dp = nn(natural(level, j), dot_t)
        ds = (p * (dp - delta)).astype(BF16)
        return nn(ds, QM[j, rows]) + nn(p.astype(BF16), DOM[j, rows]), nn(KVT[level, j, 0:64], ds)

    def out_copy(i, src, row, n, k):
        return pltpu.make_async_remote_copy(
            src_ref=src.at[head_peer(k)], dst_ref=out_ref.at[h, pl.ds(row, n)],
            send_sem=out_ss.at[i * 7 + k - 1], recv_sem=out_rs.at[i * 7 + k - 1],
            device_id={"head": head_peer(k)}, device_id_type=MESH)

    def out_local(i, src, row, n):
        return pltpu.make_async_copy(src.at[h], out_ref.at[h, pl.ds(row, n)], out_loc.at[i])

    def og_part(row, n):
        return og.at[:, pl.ds(row, n)]

    parts = []
    for j in range(2):
        parts += [(ROW_Q[j][0], 64), (ROW_Q[j][1], 64), (ROW_KV[j] + 16, 48), (ROW_KV[j], 16),
                  (ROW_KV[j] + 64, 64)]

    def start_out(i):
        row, n = parts[i]
        for k in range(1, NH):
            out_copy(i, og_part(row, n), row, n, k).start()
        out_local(i, og_part(row, n), row, n).start()

    def tz_copy(k):
        return pltpu.make_async_remote_copy(
            src_ref=og.at[head_peer(k), pl.ds(ROW_TZ, 16)], dst_ref=out_ref.at[h, pl.ds(ROW_TZ, 16)],
            send_sem=tz_ss.at[k], recv_sem=tz_rs.at[k],
            device_id={"seq": zpeer, "head": head_peer(k)}, device_id_type=MESH)

    def send_rows(i, top, bottom):
        row = parts[i][0]
        both = jnp.concatenate([top, bottom], axis=0).T.astype(BF16)
        og[:, row:row + 16] = both[0:128].reshape(8, 16, 128)
        og[:, row + 16:row + 64] = both[128:512].reshape(8, 48, 128)
        start_out(i)

    def g32_copy(j, k):
        return pltpu.make_async_remote_copy(
            src_ref=g32.at[j, k], dst_ref=r32.at[j, 16 - k],
            send_sem=l32_ss.at[29 + 15 * j + k], recv_sem=l32_rs.at[29 + 15 * j + k],
            device_id={"seq": plane_peer(k)}, device_id_type=MESH)

    def g8_copy(j, k):
        return pltpu.make_async_remote_copy(
            src_ref=g8.at[j, k], dst_ref=r8.at[j, 8 - k],
            send_sem=l8_ss.at[13 + 7 * j + k], recv_sem=l8_rs.at[13 + 7 * j + k],
            device_id={"seq": oct_peer(k)}, device_id_type=MESH)

    def g2_copy(j):
        return pltpu.make_async_remote_copy(
            src_ref=g2.at[j], dst_ref=r2.at[j], send_sem=l2_ss.at[2 + j], recv_sem=l2_rs.at[2 + j],
            device_id={"seq": pair}, device_id_type=MESH)

    def put(j):
        row, col = iota((128, 32), 0), iota((128, 32), 1)
        return (row == (col >> 2) * 16 + (col & 3) + 4 * j).astype(F32).astype(BF16)

    def spread(j, x):
        hi = x.astype(BF16)
        return nn(put(j), hi) + nn(put(j), (x - hi.astype(F32)).astype(BF16))

    def send_keys(j):
        g2_copy(j).wait()
        for b in range(8):
            t2 = ACC[1, j, b * 64 + 16:b * 64 + 64] + r2[j, b, 16:64].astype(F32)
            own = ACC[0, j, b * 128 + 16:b * 128 + 64]
            og[b, ROW_KV[j] + 16:ROW_KV[j] + 64] = (own + t2).astype(BF16)
        start_out(5 * j + 2)

    def send_other_keys(j):
        for b in range(8):
            og[b, ROW_KV[j] + 64:ROW_KV[j] + 128] = ACC[0, j, b * 128 + 64:b * 128 + 128].astype(BF16)
        start_out(5 * j + 4)

    def sum_plane(j):
        for k in range(1, 16):
            g32_copy(j, k).wait()
        total = ACC[3, j, 0:64]
        for m in range(1, 16):
            total += r32[j, m].reshape(64, 128).astype(F32)
        ACC[3, j, 0:64] = total

    def send_tiles(j):
        for k in range(1, 8):
            g8_copy(j, k).wait()
        t8 = ACC[2, j, 0:128] + spread(0, ACC[3, j, 0:32])
        for m in range(1, 8):
            t8 += r8[j, m].astype(F32)
        for b in range(8):
            t2 = ACC[1, j, b * 64:b * 64 + 16] + r2[j, b, 0:16].astype(F32)
            own = ACC[0, j, b * 128:b * 128 + 16]
            og[b, ROW_KV[j]:ROW_KV[j] + 16] = (own + t2 + t8[b * 16:b * 16 + 16]).astype(BF16)
        start_out(5 * j + 3)

    def send_plane():
        both = spread(0, ACC[3, 0, 32:64]) + spread(1, ACC[3, 1, 32:64])
        og[:, ROW_TZ:ROW_TZ + 16] = both.astype(BF16).reshape(8, 16, 128)
        for k in range(NH):
            tz_copy(k).start()

    def prepare_local(j):
        prepare(0, j, lambda c: inbuf[2 * j, c])

    def row_delta(j, part, o):
        return jnp.sum(wide(DOT, j, part)[64:128].astype(F32) * o, axis=0, keepdims=True)

    def attend_other(j):
        prepare_queries(j, 1)
        _, total, o = forward(0, j, wide(QXT, j, 1), WB)
        factor = 1.0 / total
        o = o * factor
        acc, dq = backward(0, j, WB, factor, row_delta(j, 1, o), wide(DOT, j, 1), slice(512, 1024))
        ACC[0, j] = acc if j == 0 else ACC[0, j] + acc
        send_rows(5 * j + 1, dq * 0.125, o)

    def attend_own(j, meanwhile):
        m1, l1, o1 = forward(0, j, wide(QXT, j, 0), W1)
        l2_copy(j).wait()
        prepare(1, j, lambda c: kv2[j, c // 4, c % 4 * 2:c % 4 * 2 + 2].reshape(128, 128))
        m2, l2, o2 = forward(1, j, wide(QXT, j, 0), W2)
        for k in range(1, 8):
            l8_copy(j, k).wait()
        prepare(2, j, lambda c: kv8[j, c].reshape(128, 128))
        m3, l3, o3 = forward(2, j, QXT[j, 0], W8)
        for k in range(1, 16):
            l32_copy(j, k).wait()
        prepare(3, j, lambda c: kv32[j, 2 * c:2 * c + 2].reshape(128, 128))
        m4, l4, o4 = forward(3, j, QXT32[j], W32)

        def on_first(x, f):
            return jnp.concatenate([f(x[:, 0:128]), x[:, 128:512]], axis=1)

        top = on_first(jnp.maximum(m1, m2), lambda x: jnp.maximum(x, jnp.maximum(m3, m4)))
        e1, e2 = jnp.exp(m1 - top), jnp.exp(m2 - top)
        e3, e4 = jnp.exp(m3 - top[:, 0:128]), jnp.exp(m4 - top[:, 0:128])
        factor = 1.0 / on_first(l1 * e1 + l2 * e2, lambda x: x + l3 * e3 + l4 * e4)
        o = on_first(o1 * e1 + o2 * e2, lambda x: x + o3 * e3 + o4 * e4) * factor
        delta = row_delta(j, 0, o)
        short = factor[:, 0:128], delta[:, 0:128]

        ACC[1, j], dq2 = backward(1, j, W2, e2 * factor, delta, wide(DOT, j, 0), slice(0, 512))
        g2[j] = ACC[1, j, 512:1024].reshape(8, 64, 128).astype(BF16)
        g2_copy(j).start()
        ACC[3, j], dq4 = backward(3, j, W32, e4 * short[0], short[1], DOT[j, 0], slice(0, 128))
        g32[j] = ACC[3, j].reshape(16, 2, 32, 128).astype(BF16)
        for k in range(1, 16):
            g32_copy(j, k).start()
        ACC[2, j], dq3 = backward(2, j, W8, e3 * short[0], short[1], DOT[j, 0], slice(0, 128))
        g8[j] = ACC[2, j].reshape(8, 128, 128).astype(BF16)
        for k in range(1, 8):
            g8_copy(j, k).start()
        meanwhile()
        acc, dq1 = backward(0, j, W1, e1 * factor, delta, wide(DOT, j, 0), slice(0, 512))
        ACC[0, j] = acc if j == 1 else ACC[0, j] + acc
        send_rows(5 * j, on_first(dq1 + dq2, lambda x: x + dq3 + dq4) * 0.125, o)

    wait_in(0)
    start_levels(0)
    wait_in(1)
    start_levels(1)
    wait_in(2)
    prepare_local(0)
    wait_in(3)
    attend_other(0)
    wait_in(4)
    prepare_queries(0, 0)
    attend_own(0, lambda: None)
    send_other_keys(0)
    wait_in(5)
    prepare_local(1)
    wait_in(6)
    prepare_queries(1, 0)
    attend_own(1, lambda: send_keys(0))
    sum_plane(0)
    send_tiles(0)
    wait_in(7)
    attend_other(1)
    send_other_keys(1)
    send_keys(1)
    sum_plane(1)
    send_plane()
    send_tiles(1)

    for i in range(8):
        for k in range(1, NH):
            in_copy(i, k).wait_send()
    for k in range(NH):
        zin_copy(k).wait_send()
        tz_copy(k).wait()
    for i, (row, n) in enumerate(parts):
        for k in range(1, NH):
            out_copy(i, og_part(row, n), row, n, k).wait()
        out_local(i, og_part(row, n), row, n).wait()


def restore_kernel(packed_ref, a_ref, q_ref, k_ref, v_ref):
    low = iota((128, 128), 1) < 64
    first4 = iota((16, 128), 0) < 4
    for g in range(NH):
        rho = iota((NB, NB), 1)
        mat = (iota((NB, NB), 0) == token_of(rho >> 6, rho & 63, g)).astype(F32).astype(BF16)
        cols = []
        for j in range(2):
            both = [packed_ref[g, row:row + 64] for row in ROW_Q[j]]
            cols.append(jnp.concatenate(both[::-1] if j else both, axis=0))
        for j in range(2):
            plane = packed_ref[g, ROW_TZ:ROW_TZ + 16].astype(F32)
            plane = jnp.where(first4, pltpu.roll(plane, 12, 0) if j else plane, 0.0)
            tile = packed_ref[g, ROW_KV[j]:ROW_KV[j] + 16].astype(F32) + plane
            own = [tile.astype(BF16), packed_ref[g, ROW_KV[j] + 16:ROW_KV[j] + 64]]
            other = [packed_ref[g, ROW_KV[j] + 64:ROW_KV[j] + 128]]
            cols.append(jnp.concatenate(other + own if j else own + other, axis=0))
        res = nn(mat, jnp.concatenate(cols, axis=1))
        here = slice(g * 128, g * 128 + 128)
        for first, second, at in ((q_ref, a_ref, 0), (k_ref, v_ref, 256)):
            x, y = res[:, at:at + 128], res[:, at + 128:at + 256]
            first[:, here] = jnp.where(low, x, pltpu.roll(y, 64, 1)).astype(BF16)
            second[:, here] = jnp.where(low, pltpu.roll(x, 64, 1), y).astype(BF16)


def body(queries, keys, values, grad_out, doc_ids):
    vmem = pl.BlockSpec(memory_space=pltpu.VMEM)
    dma = pltpu.SemaphoreType.DMA
    packed = pl.pallas_call(
        attend_kernel,
        out_shape=pltpu.VMEM((NH, ROWS, 128), BF16),
        in_specs=[pl.BlockSpec(memory_space=pl.ANY)] * 5,
        out_specs=vmem,
        scratch_shapes=[pltpu.VMEM(queries.shape, BF16)] * 4 + [
            pltpu.VMEM((256, 128), I32),
            pltpu.VMEM((4, NH, NB, 128), BF16),
            pltpu.VMEM((NH, 16, 128), BF16),
            pltpu.VMEM((4, NH, NB, 128), BF16),
            pltpu.VMEM((NH, 16, 128), BF16),
            pltpu.VMEM((2, 2, 8, 64, 128), BF16),
            pltpu.VMEM((2, 8, 8, 16, 128), BF16),
            pltpu.VMEM((2, 16, 2, 32, 128), BF16),
            pltpu.VMEM((4, 2, 1024, 128), BF16),
            pltpu.VMEM((4, 2, 128, 1024), BF16),
            pltpu.VMEM((512, 128), BF16),
            pltpu.VMEM((2, 8, 128, 128), BF16),
            pltpu.VMEM((2, 128, 128), BF16),
            pltpu.VMEM((2, 1024, 128), BF16),
            pltpu.VMEM((2, 1024, 128), BF16),
            pltpu.VMEM((2, 8, 128, 128), BF16),
            pltpu.VMEM((1024, 512), F32),
            pltpu.VMEM((1024, 512), F32),
            pltpu.VMEM((1024, 512), F32),
            pltpu.VMEM((1024, 128), F32),
            pltpu.VMEM((1024, 128), F32),
            pltpu.VMEM((4, 2, 1024, 128), F32),
            pltpu.VMEM((2, 8, 64, 128), BF16),
            pltpu.VMEM((2, 8, 64, 128), BF16),
            pltpu.VMEM((2, 8, 128, 128), BF16),
            pltpu.VMEM((2, 8, 128, 128), BF16),
            pltpu.VMEM((2, 16, 2, 32, 128), BF16),
            pltpu.VMEM((2, 16, 2, 32, 128), BF16),
            pltpu.VMEM((NH, ROWS, 128), BF16),
            dma((5,)), dma((56,)), dma((56,)), dma((8,)), dma((8,)), dma((8,)),
            dma((4,)), dma((4,)), dma((28,)), dma((28,)), dma((60,)), dma((60,)),
            dma((70,)), dma((70,)), dma((8,)), dma((8,)), dma((10,)),
        ],
        compiler_params=pltpu.CompilerParams(
            collective_id=0, has_side_effects=True, vmem_limit_bytes=56 * 1024 * 1024),
        name="attend",
    )(queries, keys, values, grad_out, doc_ids.reshape(256, 128))
    shape = jax.ShapeDtypeStruct(queries.shape, BF16)
    return pl.pallas_call(
        restore_kernel,
        out_shape=(shape, shape, shape, shape),
        in_specs=[vmem],
        out_specs=(vmem, vmem, vmem, vmem),
        compiler_params=pltpu.CompilerParams(vmem_limit_bytes=32 * 1024 * 1024),
        name="restore",
    )(packed)


def solution(mesh):
    spec = P(("seq", "head"), None)
    return jax.shard_map(
        body, mesh=mesh, in_specs=(spec, spec, spec, spec, P()), out_specs=(spec, spec, spec, spec), check_vma=False)
```
